128 devices in a mesh: line: 8 (over x_hi, z), out: 16 (over x_lo, y, core).
Axes of the slice: x: 4 (x_hi: 2, x_lo: 2; x = x_hi * 2 + x_lo), y: 4, z: 4, core: 2. Of those that a mesh axis runs over, the one named last changes fastest.
Arguments:
- injections: bfloat16 [32, 8192], P(None, 'out'), may hold values from -6 to 6
- shift_factors: bfloat16 [16384, 8192], P('line', 'out'), may hold values from -0.0625 to 0.0625
- outage_factors: bfloat16 [16384, 16384], P('out', 'line'), may hold values from -3 to 3
- limits: float32 [16384], P('line'), may hold values from 0.6 to 1.6
- outage_line: int32 [16384], P('out'), may hold values from 0 to 16383, each once
- tile_list: int32 [16, 16], P('out'), may hold values from 0 to 15, as said below
- tile_count: int32 [16], P('out'), may hold values from 1 to 16, as said below
Outputs:
- injection_grad: float32 [32, 8192], P(None, 'out')
The draws below stay inside these ranges and needn't reach their ends.
Inputs may be any that keep to these rules, and one draw needn't show every extreme that they name: `outage_line`: each line is taken out by exactly one outage. `tile_list`: each row names every one of its 16 local tiles once, in an order drawn from the seed. `tile_count`: some index of out has all its tiles screened in.
All inputs are finite; a program needn't handle non-finite values.
Results may differ from the reference program's by a relative error of at most 0.0018.
Values may be sent and summed in bfloat16 or wider, within the bound.
A program may use at most 64 MiB of HBM per device.

```python
import jax
import jax.numpy as jnp
from jax import lax

CASES = 32
NI = 8192
NL = 16384
TILE = 64
NO = 16384
OD = 1024
OT_DEV = 16


def draw_tile_list(key, part):
    groups = NO // OD
    key_rows = jax.random.split(jax.random.fold_in(key, 11), groups)
    return jax.vmap(lambda one_key: jax.random.permutation(one_key, OT_DEV))(key_rows).astype(jnp.int32)


def draw_tile_count(key, part):
    groups = NO // OD
    counts = jax.random.randint(jax.random.fold_in(key, 21), (groups,), 1, OT_DEV + 1)
    fullest = jax.random.randint(jax.random.fold_in(key, 22), (), 0, groups)
    return counts.at[fullest].set(OT_DEV).astype(jnp.int32)


def shard_levels(rng, extent, cuts, least, largest):
    def one(dim, shards_of):
        draws = jax.random.uniform(jax.random.fold_in(jax.random.fold_in(rng, 6), dim), (shards_of,), jnp.float32, least / len(cuts), largest / len(cuts))
        return jnp.repeat(jnp.exp(draws), extent[dim] // shards_of).reshape((-1,) + (1,) * (len(extent) - dim - 1))

    factor_of = one(*cuts[0])
    for cut in cuts[1:]:
        factor_of = factor_of * one(*cut)
    return factor_of


def gaussian(rng, shape, deviation, bound, cuts=(), kind=jnp.bfloat16):
    level = shard_levels(rng, shape, cuts, -0.22, 0.18) if cuts else 1.0
    result = jax.random.normal(rng, shape, jnp.float32) * deviation * level
    return jnp.minimum(jnp.maximum(result, -bound), bound).astype(kind)


def setup_inputs(seed: int = 0) -> dict:
    streams_of = jax.random.split(jax.random.key(seed), 8)
    injections = gaussian(streams_of[0], (CASES, NI), 1.0, 6.0, ((1, 16),))
    shift_factors = gaussian(streams_of[1], (NL, NI), NI ** -0.5, 0.0625, ((0, 8), (1, 16)))
    outage_factors = gaussian(streams_of[2], (NO, NL), 0.5, 3.0, ((0, 16), (1, 8)))
    limits = jnp.clip(0.6 + 1.0 * jax.random.uniform(streams_of[3], (NL,), jnp.float32) ** shard_levels(streams_of[3], (NL,), ((0, 8),), -0.2, 0.2), 0.6, 1.6)
    outage_line = jax.random.permutation(streams_of[4], NL).astype(jnp.int32)
    tile_list = draw_tile_list(jax.random.fold_in(streams_of[7], 71), 0)
    tile_count = draw_tile_count(jax.random.fold_in(streams_of[7], 71), 0)
    return {"injections": injections, "shift_factors": shift_factors, "outage_factors": outage_factors, "limits": limits, "outage_line": outage_line, "tile_list": tile_list, "tile_count": tile_count}


def reference(injections, shift_factors, outage_factors, limits, outage_line, tile_list, tile_count):
    line_flows = lax.dot_general(injections, shift_factors, (((1,), (1,)), ((), ())), preferred_element_type=jnp.float32)
    fall_flows = jnp.take(line_flows, outage_line, axis=1)
    position = jnp.arange(OT_DEV, dtype=jnp.int32)
    listed = (position[None, :] < tile_count[:, None]).astype(jnp.float32)
    match_table = (tile_list[:, :, None] == position[None, None, :]).astype(jnp.float32)
    screened = jnp.sum(match_table * listed[:, :, None], axis=1)
    block_mask = screened.reshape(-1)
    weight_scale = 2.0 / NO
    blocks = NO // TILE
    factor_blocks = outage_factors.reshape(blocks, TILE, NL)
    fall_blocks = fall_flows.reshape(CASES, blocks, TILE).transpose(1, 0, 2)

    def block_step(direct, pieces):
        factors, fallen_block, active = pieces
        factors_wide = factors.astype(jnp.float32)
        post_flow = line_flows[:, None, :] + fallen_block[:, :, None] * factors_wide[None]
        excess = jnp.maximum(jnp.abs(post_flow) - limits[None, None, :], 0.0)
        slope = (weight_scale * active) * excess * jnp.sign(post_flow)
        return direct + jnp.sum(slope, axis=1), jnp.sum(slope * factors_wide[None], axis=2)

    direct, reverse = lax.scan(block_step, jnp.zeros((CASES, NL), jnp.float32), (factor_blocks, fall_blocks, block_mask))
    reverse = reverse.transpose(1, 0, 2).reshape(CASES, NO)
    grad_flow = direct.at[:, outage_line].add(reverse)
    return jnp.dot(grad_flow.astype(jnp.bfloat16), shift_factors, preferred_element_type=jnp.float32)
```

```python
import functools

import jax
import jax.numpy as jnp
from jax import lax
from jax.experimental import pallas as pl
from jax.experimental.pallas import tpu as pltpu
from jax.sharding import PartitionSpec as P

CASES = 32
NO = 16384
TILE = 64
LB = 128
F32 = jnp.float32
BF16 = jnp.bfloat16
MESH = pl.DeviceIdType.MESH
VMEM = pl.BlockSpec(memory_space=pltpu.VMEM)
SMEM = pl.BlockSpec(memory_space=pltpu.SMEM)


def peer(axis, size, offset):
    if axis == "out":
        return (lax.axis_index("line"), lax.rem(lax.axis_index("out") + offset, size))
    return (lax.rem(lax.axis_index("line") + offset, size), lax.axis_index("out"))


def greet(n_line, n_out):
    barrier = pltpu.get_barrier_semaphore()
    for i in range(1, n_out):
        pl.semaphore_signal(barrier, inc=1, device_id=peer("out", n_out, i), device_id_type=MESH)
    for i in range(1, n_line):
        pl.semaphore_signal(barrier, inc=1, device_id=peer("line", n_line, i), device_id_type=MESH)
    return barrier


def send(src, dst, sems, i, axis, size):
    copy = pltpu.make_async_remote_copy(
        src_ref=src,
        dst_ref=dst,
        send_sem=sems.at[0, i],
        recv_sem=sems.at[1, i],
        device_id=peer(axis, size, i),
        device_id_type=MESH,
    )
    copy.start()
    return copy


def split3(x):
    hi = x.astype(BF16)
    rest = x - hi.astype(F32)
    mid = rest.astype(BF16)
    low = (rest - mid.astype(F32)).astype(BF16)
    return jnp.concatenate([hi, mid, low], axis=0)


def scatter_sum(parts, recv, sems, axis, size, fill=None):
    me = lax.axis_index(axis)
    copies = []
    for i in range(1, size):
        d = lax.rem(me + i, size)
        if fill is not None:
            fill(d)
        copies.append(send(parts.at[d], recv.at[i], sems, i, axis, size))
    if fill is not None:
        fill(me)
    total = parts[me]
    for i in range(1, size):
        copies[i - 1].wait_recv()
        total = total + recv[i]
    for copy in copies:
        copy.wait_send()
    return total


def spread(slots, sems, axis, size):
    me = lax.axis_index(axis)
    copies = [send(slots.at[me], slots.at[me], sems, i, axis, size) for i in range(1, size)]
    for copy in copies:
        copy.wait_recv()
    for copy in copies:
        copy.wait_send()


def flows_kernel(
    n_line, n_out, inj_ref, sf_ref, line_ref, lf_ref, ff_ref,
    parts, recv_o, slots_o, hot, picked, recv_l, slots_l, s_ro, s_go, s_rl, s_gl,
):
    barrier = greet(n_line, n_out)
    line_start = lax.axis_index("line") * (n_out * LB)
    n_k = n_line * LB

    def fill(d):
        rows = sf_ref[pl.ds(pl.multiple_of(d * LB, LB), LB), :]
        parts[d] = lax.dot_general(
            inj_ref[...], rows, (((1,), (1,)), ((), ())), preferred_element_type=F32
        )

    pl.semaphore_wait(barrier, n_out + n_line - 2)
    me_out = lax.axis_index("out")
    me_line = lax.axis_index("line")
    copies = []
    for i in range(1, n_out):
        d = lax.rem(me_out + i, n_out)
        fill(d)
        copies.append(send(parts.at[d], recv_o.at[i], s_ro, i, "out", n_out))
    fill(me_out)
    local = line_ref[...] - line_start

    def hot_rows(r, _):
        base = pl.multiple_of(r * LB, LB)
        ids = lax.broadcasted_iota(jnp.int32, (LB, n_k), 0) + base
        hot[pl.ds(base, LB), :] = (ids == local).astype(F32).astype(BF16)
        return 0

    lax.fori_loop(0, n_out, hot_rows, 0)
    total = parts[me_out]
    for i in range(1, n_out):
        copies[i - 1].wait_recv()
        total = total + recv_o[i]
    slots_o[me_out] = total
    spread(slots_o, s_go, "out", n_out)
    for copy in copies:
        copy.wait_send()
    lf_ref[...] = slots_o[...]

    wide = jnp.concatenate([slots_o[i] for i in range(n_out)], axis=1)
    got = jnp.dot(split3(wide), hot[...], preferred_element_type=F32)
    got = got[:CASES] + got[CASES : 2 * CASES] + got[2 * CASES :]
    for i in range(n_line):
        picked[i] = got[:, i * LB : (i + 1) * LB]
    slots_l[me_line] = scatter_sum(picked, recv_l, s_rl, "line", n_line)
    spread(slots_l, s_gl, "line", n_line)
    ff_ref[...] = slots_l[...]


def flows(n_line, n_out, injections, shift_factors, outage_line):
    n_k = n_line * LB
    block = (CASES, LB)
    dma = pltpu.SemaphoreType.DMA
    return pl.pallas_call(
        functools.partial(flows_kernel, n_line, n_out),
        in_specs=[VMEM, VMEM, VMEM],
        out_specs=[VMEM, VMEM],
        out_shape=[
            jax.ShapeDtypeStruct((n_out,) + block, F32),
            jax.ShapeDtypeStruct((n_line,) + block, F32),
        ],
        scratch_shapes=[
            pltpu.VMEM((n_out,) + block, F32),
            pltpu.VMEM((n_out,) + block, F32),
            pltpu.VMEM((n_out,) + block, F32),
            pltpu.VMEM((n_out * LB, n_k), BF16),
            pltpu.VMEM((n_line,) + block, F32),
            pltpu.VMEM((n_line,) + block, F32),
            pltpu.VMEM((n_line,) + block, F32),
            dma((2, n_out)),
            dma((2, n_out)),
            dma((2, n_line)),
            dma((2, n_line)),
        ],
        compiler_params=pltpu.CompilerParams(
            collective_id=0, has_side_effects=True, vmem_limit_bytes=40 * 2**20
        ),
        name="flows",
    )(injections, shift_factors, outage_line.reshape(1, n_k))


def terms_kernel(
    n_line, n_out, list_ref, count_ref, of_ref, lf_ref, lim_ref, ff_ref, dir_ref, rev_ref,
    wide_of, low, high, fall, dsum, qsum, rtile,
):
    n_l = n_out * LB
    for t in range(n_out):
        cols = pl.ds(t * LB, LB)
        lim = lim_ref[:, cols]
        flow = lf_ref[t]
        for c in range(CASES):
            low[c, :, cols] = jnp.broadcast_to(-lim - flow[c : c + 1], (8, LB))
            high[c, :, cols] = jnp.broadcast_to(lim - flow[c : c + 1], (8, LB))
    dsum[...] = jnp.zeros_like(dsum)
    qsum[...] = jnp.zeros_like(qsum)
    rtile[...] = jnp.zeros_like(rtile)

    def fall_block(kb, _):
        turned = ff_ref[kb].T
        rows = pl.ds(pl.multiple_of(kb * LB, LB), LB)
        for c in range(CASES):
            fall[c, rows, :] = jnp.broadcast_to(turned[:, c : c + 1], (LB, LB))
        return 0

    lax.fori_loop(0, n_line, fall_block, 0)
    ones = jnp.ones((8, LB), F32)

    def tile_step(step, _):
        tile = list_ref[0, step]
        k0 = pl.multiple_of(tile * TILE, TILE)
        narrow = of_ref[pl.ds(k0, TILE), :]
        wide_of[...] = narrow.astype(F32)
        pair = ff_ref[tile // 2]
        half = lax.rem(tile, 2) == 0
        mine = jnp.where(half, pair[:, :TILE], pair[:, TILE:])
        prod = jnp.dot(split3(mine), narrow, preferred_element_type=F32)
        qsum[...] += prod[:CASES] + prod[CASES : 2 * CASES] + prod[2 * CASES :]
        square = jnp.zeros((TILE, LB), F32)
        for t in range(n_out):
            w = wide_of[:, t * LB : (t + 1) * LB]
            square = square + w * w

        def case_step(c, _):
            ffs = [fall[c, pl.ds(k0 + 8 * i, 8), :] for i in range(TILE // 8)]
            acc = [ffs[i] * square[8 * i : 8 * i + 8] for i in range(TILE // 8)]
            for t in range(n_out):
                cols = pl.ds(t * LB, LB)
                lo = low[c, :, cols]
                hi = high[c, :, cols]
                total = None
                for i in range(TILE // 8):
                    o = wide_of[8 * i : 8 * i + 8, t * LB : (t + 1) * LB]
                    q = jnp.minimum(jnp.maximum(ffs[i] * o, lo), hi)
                    acc[i] = acc[i] - q * o
                    total = q if total is None else total + q
                dsum[c, :, cols] += total
            row = lax.dot_general(
                ones, jnp.concatenate(acc, axis=0), (((1,), (1,)), ((), ())),
                precision=lax.Precision.HIGHEST, preferred_element_type=F32,
            )
            rtile[tile, pl.ds(c, 1), 0:TILE] = row[0:1]
            return 0

        lax.fori_loop(0, CASES, case_step, 0)
        return 0

    lax.fori_loop(0, count_ref[0], tile_step, 0)
    for t in range(n_out):
        cols = slice(t * LB, (t + 1) * LB)
        dir_ref[t] = qsum[:, cols] - jnp.sum(dsum[:, :, cols], axis=1)
    for b in range(n_line):
        rev_ref[b] = jnp.concatenate([rtile[2 * b, :, :TILE], rtile[2 * b + 1, :, :TILE]], axis=1)


def terms(n_line, n_out, tile_list, tile_count, outage_factors, lf, limits, ff):
    n_l = n_out * LB
    n_k = n_line * LB
    block = (CASES, LB)
    return pl.pallas_call(
        functools.partial(terms_kernel, n_line, n_out),
        in_specs=[SMEM, SMEM, VMEM, VMEM, VMEM, VMEM],
        out_specs=[VMEM, VMEM],
        out_shape=[
            jax.ShapeDtypeStruct((n_out,) + block, F32),
            jax.ShapeDtypeStruct((n_line,) + block, F32),
        ],
        scratch_shapes=[
            pltpu.VMEM((TILE, n_l), F32),
            pltpu.VMEM((CASES, 8, n_l), F32),
            pltpu.VMEM((CASES, 8, n_l), F32),
            pltpu.VMEM((CASES, n_k, LB), F32),
            pltpu.VMEM((CASES, 8, n_l), F32),
            pltpu.VMEM((CASES, n_l), F32),
            pltpu.VMEM((n_k // TILE, CASES, LB), F32),
        ],
        compiler_params=pltpu.CompilerParams(vmem_limit_bytes=56 * 2**20),
        name="terms",
    )(tile_list, tile_count, outage_factors, lf, limits.reshape(1, n_l), ff)


def grads_kernel(
    n_line, n_out, dir_ref, rev_ref, line_ref, sf_ref, out_ref,
    recv_r, slots_r, hot, parts, recv_o, slots_o, shares, recv_f, slots_f,
    s_rr, s_gr, s_ro, s_go, s_rf, s_gf,
):
    barrier = greet(n_line, n_out)
    me_line = lax.axis_index("line")
    me_out = lax.axis_index("out")
    line_start = me_line * (n_out * LB)
    n_k = n_line * LB
    pl.semaphore_wait(barrier, n_out + n_line - 2)
    copies = []
    for i in range(1, n_line):
        d = lax.rem(me_line + i, n_line)
        copies.append(send(rev_ref.at[d], recv_r.at[i], s_rr, i, "line", n_line))
    local = line_ref[...] - line_start

    def hot_rows(r, _):
        base = pl.multiple_of(r * LB, LB)
        ids = lax.broadcasted_iota(jnp.int32, (LB, n_k), 0) + base
        hot[pl.ds(base, LB), :] = (ids == local).astype(F32).astype(BF16)
        return 0

    lax.fori_loop(0, n_out, hot_rows, 0)
    total = rev_ref[me_line]
    for i in range(1, n_line):
        copies[i - 1].wait_recv()
        total = total + recv_r[i]
    slots_r[me_line] = total
    spread(slots_r, s_gr, "line", n_line)
    for copy in copies:
        copy.wait_send()
    three = split3(jnp.concatenate([slots_r[i] for i in range(n_line)], axis=1))

    def fill(d):
        table = hot[pl.ds(pl.multiple_of(d * LB, LB), LB), :]
        got = lax.dot_general(three, table, (((1,), (1,)), ((), ())), preferred_element_type=F32)
        parts[d] = dir_ref[d] + (got[:CASES] + got[CASES : 2 * CASES] + got[2 * CASES :])

    grad = scatter_sum(parts, recv_o, s_ro, "out", n_out, fill)
    slots_o[me_out] = (grad * (2.0 / NO)).astype(BF16)
    spread(slots_o, s_go, "out", n_out)
    rounded = jnp.concatenate([slots_o[i] for i in range(n_out)], axis=1)
    partial = jnp.dot(rounded, sf_ref[...], preferred_element_type=F32)
    half = CASES // 2
    for i in range(n_line):
        r, q = i % 2, i // 2
        shares[i] = partial[r * half : (r + 1) * half, q * LB : (q + 1) * LB]
    slots_f[me_line] = scatter_sum(shares, recv_f, s_rf, "line", n_line)
    spread(slots_f, s_gf, "line", n_line)
    for i in range(n_line):
        r, q = i % 2, i // 2
        out_ref[r * half : (r + 1) * half, q * LB : (q + 1) * LB] = slots_f[i]


def grads(n_line, n_out, direct, reverse, outage_line, shift_factors):
    n_k = n_line * LB
    block = (CASES, LB)
    share = (n_line, CASES // 2, LB)
    dma = pltpu.SemaphoreType.DMA
    return pl.pallas_call(
        functools.partial(grads_kernel, n_line, n_out),
        in_specs=[VMEM] * 4,
        out_specs=VMEM,
        out_shape=jax.ShapeDtypeStruct((CASES, shift_factors.shape[1]), F32),
        scratch_shapes=[
            pltpu.VMEM((n_line,) + block, F32),
            pltpu.VMEM((n_line,) + block, F32),
            pltpu.VMEM((n_out * LB, n_k), BF16),
            pltpu.VMEM((n_out,) + block, F32),
            pltpu.VMEM((n_out,) + block, F32),
            pltpu.VMEM((n_out,) + block, BF16),
            pltpu.VMEM(share, F32),
            pltpu.VMEM(share, F32),
            pltpu.VMEM(share, F32),
            dma((2, n_line)),
            dma((2, n_line)),
            dma((2, n_out)),
            dma((2, n_out)),
            dma((2, n_line)),
            dma((2, n_line)),
        ],
        compiler_params=pltpu.CompilerParams(
            collective_id=1, has_side_effects=True, vmem_limit_bytes=40 * 2**20
        ),
        name="grads",
    )(direct, reverse, outage_line.reshape(1, n_k), shift_factors)


def shards(
    n_line, n_out, injections, shift_factors, outage_factors, limits, outage_line, tile_list, tile_count
):
    lf, ff = flows(n_line, n_out, injections, shift_factors, outage_line)
    direct, reverse = terms(n_line, n_out, tile_list, tile_count, outage_factors, lf, limits, ff)
    return grads(n_line, n_out, direct, reverse, outage_line, shift_factors)


def solution(mesh):
    placed = (
        P(None, "out"),
        P("line", "out"),
        P("out", "line"),
        P("line"),
        P("out"),
        P("out", None),
        P("out"),
    )
    return jax.shard_map(
        functools.partial(shards, mesh.shape["line"], mesh.shape["out"]),
        mesh=mesh,
        in_specs=placed,
        out_specs=P(None, "out"),
        check_vma=False,
    )
```

```python
import functools

import jax
import jax.numpy as jnp
from jax import lax
from jax.experimental import pallas as pl
from jax.experimental.pallas import tpu as pltpu
from jax.sharding import PartitionSpec as P

CASES = 32
NO = 16384
TILE = 64
LB = 128
F32 = jnp.float32
BF16 = jnp.bfloat16
MESH = pl.DeviceIdType.MESH
VMEM = pl.BlockSpec(memory_space=pltpu.VMEM)
SMEM = pl.BlockSpec(memory_space=pltpu.SMEM)


def peer(axis, size, offset):
    if axis == "out":
        return (lax.axis_index("line"), lax.rem(lax.axis_index("out") + offset, size))
    return (lax.rem(lax.axis_index("line") + offset, size), lax.axis_index("out"))


def greet(n_line, n_out):
    barrier = pltpu.get_barrier_semaphore()
    for i in range(1, n_out):
        pl.semaphore_signal(barrier, inc=1, device_id=peer("out", n_out, i), device_id_type=MESH)
    for i in range(1, n_line):
        pl.semaphore_signal(barrier, inc=1, device_id=peer("line", n_line, i), device_id_type=MESH)
    return barrier


def send(src, dst, sems, i, axis, size):
    copy = pltpu.make_async_remote_copy(
        src_ref=src,
        dst_ref=dst,
        send_sem=sems.at[0, i],
        recv_sem=sems.at[1, i],
        device_id=peer(axis, size, i),
        device_id_type=MESH,
    )
    copy.start()
    return copy


def split3(x):
    hi = x.astype(BF16)
    rest = x - hi.astype(F32)
    mid = rest.astype(BF16)
    low = (rest - mid.astype(F32)).astype(BF16)
    return jnp.concatenate([hi, mid, low], axis=0)


def scatter_sum(parts, recv, sems, axis, size, fill=None):
    me = lax.axis_index(axis)
    copies = []
    for i in range(1, size):
        d = lax.rem(me + i, size)
        if fill is not None:
            fill(d)
        copies.append(send(parts.at[d], recv.at[i], sems, i, axis, size))
    if fill is not None:
        fill(me)
    total = parts[me]
    for i in range(1, size):
        copies[i - 1].wait_recv()
        total = total + recv[i]
    for copy in copies:
        copy.wait_send()
    return total


def spread(slots, sems, axis, size):
    me = lax.axis_index(axis)
    copies = [send(slots.at[me], slots.at[me], sems, i, axis, size) for i in range(1, size)]
    for copy in copies:
        copy.wait_recv()
    for copy in copies:
        copy.wait_send()


def flows_kernel(
    n_line, n_out, inj_ref, sf_ref, line_ref, lf_ref, ff_ref,
    parts, recv_o, slots_o, hot, picked, recv_l, slots_l, s_ro, s_go, s_rl, s_gl,
):
    barrier = greet(n_line, n_out)
    line_start = lax.axis_index("line") * (n_out * LB)
    n_k = n_line * LB

    def fill(d):
        rows = sf_ref[pl.ds(pl.multiple_of(d * LB, LB), LB), :]
        parts[d] = lax.dot_general(
            inj_ref[...], rows, (((1,), (1,)), ((), ())), preferred_element_type=F32
        )

    pl.semaphore_wait(barrier, n_out + n_line - 2)
    me_out = lax.axis_index("out")
    me_line = lax.axis_index("line")
    copies = []
    for i in range(1, n_out):
        d = lax.rem(me_out + i, n_out)
        fill(d)
        copies.append(send(parts.at[d], recv_o.at[i], s_ro, i, "out", n_out))
    fill(me_out)
    local = line_ref[...] - line_start

    def hot_rows(r, _):
        base = pl.multiple_of(r * LB, LB)
        ids = lax.broadcasted_iota(jnp.int32, (LB, n_k), 0) + base
        hot[pl.ds(base, LB), :] = (ids == local).astype(F32).astype(BF16)
        return 0

    lax.fori_loop(0, n_out, hot_rows, 0)
    total = parts[me_out]
    for i in range(1, n_out):
        copies[i - 1].wait_recv()
        total = total + recv_o[i]
    slots_o[me_out] = total
    spread(slots_o, s_go, "out", n_out)
    for copy in copies:
        copy.wait_send()
    lf_ref[...] = slots_o[...]

    wide = jnp.concatenate([slots_o[i] for i in range(n_out)], axis=1)
    got = jnp.dot(split3(wide), hot[...], preferred_element_type=F32)
    got = got[:CASES] + got[CASES : 2 * CASES] + got[2 * CASES :]
    for i in range(n_line):
        picked[i] = got[:, i * LB : (i + 1) * LB]
    slots_l[me_line] = scatter_sum(picked, recv_l, s_rl, "line", n_line)
    spread(slots_l, s_gl, "line", n_line)
    ff_ref[...] = slots_l[...]


def flows(n_line, n_out, injections, shift_factors, outage_line):
    n_k = n_line * LB
    block = (CASES, LB)
    dma = pltpu.SemaphoreType.DMA
    return pl.pallas_call(
        functools.partial(flows_kernel, n_line, n_out),
        in_specs=[VMEM, VMEM, VMEM],
        out_specs=[VMEM, VMEM],
        out_shape=[
            jax.ShapeDtypeStruct((n_out,) + block, F32),
            jax.ShapeDtypeStruct((n_line,) + block, F32),
        ],
        scratch_shapes=[
            pltpu.VMEM((n_out,) + block, F32),
            pltpu.VMEM((n_out,) + block, F32),
            pltpu.VMEM((n_out,) + block, F32),
            pltpu.VMEM((n_out * LB, n_k), BF16),
            pltpu.VMEM((n_line,) + block, F32),
            pltpu.VMEM((n_line,) + block, F32),
            pltpu.VMEM((n_line,) + block, F32),
            dma((2, n_out)),
            dma((2, n_out)),
            dma((2, n_line)),
            dma((2, n_line)),
        ],
        compiler_params=pltpu.CompilerParams(
            collective_id=0, has_side_effects=True, vmem_limit_bytes=40 * 2**20
        ),
        name="flows",
    )(injections, shift_factors, outage_line.reshape(1, n_k))


def terms_kernel(
    n_line, n_out, list_ref, count_ref, of_ref, lf_ref, lim_ref, ff_ref, dir_ref, rev_ref,
    wide_of, low, high, fall, dsum, qsum, turned, rsum,
):
    for t in range(n_out):
        cols = pl.ds(t * LB, LB)
        lim = lim_ref[:, cols]
        flow = lf_ref[t]
        for c in range(CASES):
            low[c, :, cols] = jnp.broadcast_to(-lim - flow[c : c + 1], (8, LB))
            high[c, :, cols] = jnp.broadcast_to(lim - flow[c : c + 1], (8, LB))
    for b in range(n_line):
        turned[b * LB : (b + 1) * LB, 0:CASES] = ff_ref[b].T
    dsum[...] = jnp.zeros_like(dsum)
    qsum[...] = jnp.zeros_like(qsum)
    rsum[...] = jnp.zeros_like(rsum)
    n_sub = TILE // 8
    lanes = lax.broadcasted_iota(jnp.int32, (8, LB), 1)

    def tile_step(step, _):
        tile = list_ref[0, step]
        k0 = pl.multiple_of(tile * TILE, TILE)
        narrow = of_ref[pl.ds(k0, TILE), :]
        wide_of[...] = narrow.astype(F32)
        pair = ff_ref[tile // 2]
        half = lax.rem(tile, 2) == 0
        mine = jnp.where(half, pair[:, :TILE], pair[:, TILE:])
        prod = jnp.dot(split3(mine), narrow, preferred_element_type=F32)
        qsum[...] += prod[:CASES] + prod[CASES : 2 * CASES] + prod[2 * CASES :]
        square = jnp.zeros((TILE, LB), F32)
        for t in range(n_out):
            w = wide_of[:, t * LB : (t + 1) * LB]
            square = square + w * w
        for c in range(CASES):
            fall[c] = jnp.broadcast_to(turned[pl.ds(k0, TILE), c : c + 1], (TILE, LB))

        def reduce_rows(c, sums):
            return tuple(
                jnp.where(lanes == c, jnp.sum(fall[jnp.maximum(c, 0), 8 * i : 8 * i + 8, :], axis=1, keepdims=True), sums[i])
                for i in range(n_sub)
            )

        def case_step(c, sums):
            sums = reduce_rows(c - 1, sums)
            ffs = [fall[c, 8 * i : 8 * i + 8, :] for i in range(n_sub)]
            acc = [ffs[i] * square[8 * i : 8 * i + 8] for i in range(n_sub)]
            for t in range(n_out):
                cols = pl.ds(t * LB, LB)
                lo = low[c, :, cols]
                hi = high[c, :, cols]
                total = None
                for i in range(n_sub):
                    o = wide_of[8 * i : 8 * i + 8, t * LB : (t + 1) * LB]
                    q = jnp.minimum(jnp.maximum(ffs[i] * o, lo), hi)
                    acc[i] = acc[i] - q * o
                    total = q if total is None else total + q
                dsum[c, :, cols] += total
            for i in range(n_sub):
                fall[c, 8 * i : 8 * i + 8, :] = acc[i]
            return sums

        zero = jnp.zeros((8, LB), F32)
        sums = lax.fori_loop(0, CASES, case_step, (zero,) * n_sub)
        sums = reduce_rows(CASES - 1, sums)
        for i in range(n_sub):
            rsum[pl.ds(k0 + 8 * i, 8), :] = sums[i]
        return 0

    lax.fori_loop(0, count_ref[0], tile_step, 0)
    for t in range(n_out):
        cols = slice(t * LB, (t + 1) * LB)
        dir_ref[t] = qsum[:, cols] - jnp.sum(dsum[:, :, cols], axis=1)
    for b in range(n_line):
        rev_ref[b] = rsum[b * LB : (b + 1) * LB, :].T[:CASES]


def terms(n_line, n_out, tile_list, tile_count, outage_factors, lf, limits, ff):
    n_l = n_out * LB
    n_k = n_line * LB
    block = (CASES, LB)
    return pl.pallas_call(
        functools.partial(terms_kernel, n_line, n_out),
        in_specs=[SMEM, SMEM, VMEM, VMEM, VMEM, VMEM],
        out_specs=[VMEM, VMEM],
        out_shape=[
            jax.ShapeDtypeStruct((n_out,) + block, F32),
            jax.ShapeDtypeStruct((n_line,) + block, F32),
        ],
        scratch_shapes=[
            pltpu.VMEM((TILE, n_l), F32),
            pltpu.VMEM((CASES, 8, n_l), F32),
            pltpu.VMEM((CASES, 8, n_l), F32),
            pltpu.VMEM((CASES, TILE, LB), F32),
            pltpu.VMEM((CASES, 8, n_l), F32),
            pltpu.VMEM((CASES, n_l), F32),
            pltpu.VMEM((n_k, LB), F32),
            pltpu.VMEM((n_k, LB), F32),
        ],
        compiler_params=pltpu.CompilerParams(vmem_limit_bytes=56 * 2**20),
        name="terms",
    )(tile_list, tile_count, outage_factors, lf, limits.reshape(1, n_l), ff)


def grads_kernel(
    n_line, n_out, dir_ref, rev_ref, line_ref, sf_ref, out_ref,
    recv_r, slots_r, hot, parts, recv_o, slots_o, slots_f,
    s_rr, s_gr, s_ro, s_go, s_gf,
):
    barrier = greet(n_line, n_out)
    me_line = lax.axis_index("line")
    me_out = lax.axis_index("out")
    line_start = me_line * (n_out * LB)
    n_k = n_line * LB
    pl.semaphore_wait(barrier, n_out + n_line - 2)
    copies = []
    for i in range(1, n_line):
        d = lax.rem(me_line + i, n_line)
        copies.append(send(rev_ref.at[d], recv_r.at[i], s_rr, i, "line", n_line))
    local = line_ref[...] - line_start

    def hot_rows(r, _):
        base = pl.multiple_of(r * LB, LB)
        ids = lax.broadcasted_iota(jnp.int32, (LB, n_k), 0) + base
        hot[pl.ds(base, LB), :] = (ids == local).astype(F32).astype(BF16)
        return 0

    lax.fori_loop(0, n_out, hot_rows, 0)
    total = rev_ref[me_line]
    for i in range(1, n_line):
        copies[i - 1].wait_recv()
        total = total + recv_r[i]
    slots_r[me_line] = total
    spread(slots_r, s_gr, "line", n_line)
    for copy in copies:
        copy.wait_send()
    three = split3(jnp.concatenate([slots_r[i] for i in range(n_line)], axis=1))

    def fill(d):
        table = hot[pl.ds(pl.multiple_of(d * LB, LB), LB), :]
        got = lax.dot_general(three, table, (((1,), (1,)), ((), ())), preferred_element_type=F32)
        parts[d] = dir_ref[d] + (got[:CASES] + got[CASES : 2 * CASES] + got[2 * CASES :])

    grad = scatter_sum(parts, recv_o, s_ro, "out", n_out, fill)
    slots_o[me_out] = (grad * (2.0 / NO)).astype(BF16)
    spread(slots_o, s_go, "out", n_out)
    rounded = jnp.concatenate([slots_o[i] for i in range(n_out)], axis=1)
    partial = jnp.dot(rounded, sf_ref[...], preferred_element_type=F32)
    slots_f[me_line] = partial.astype(BF16)
    spread(slots_f, s_gf, "line", n_line)
    result = slots_f[0].astype(F32)
    for i in range(1, n_line):
        result = result + slots_f[i].astype(F32)
    out_ref[...] = result


def grads(n_line, n_out, direct, reverse, outage_line, shift_factors):
    n_k = n_line * LB
    block = (CASES, LB)
    dma = pltpu.SemaphoreType.DMA
    return pl.pallas_call(
        functools.partial(grads_kernel, n_line, n_out),
        in_specs=[VMEM] * 4,
        out_specs=VMEM,
        out_shape=jax.ShapeDtypeStruct((CASES, shift_factors.shape[1]), F32),
        scratch_shapes=[
            pltpu.VMEM((n_line,) + block, F32),
            pltpu.VMEM((n_line,) + block, F32),
            pltpu.VMEM((n_out * LB, n_k), BF16),
            pltpu.VMEM((n_out,) + block, F32),
            pltpu.VMEM((n_out,) + block, F32),
            pltpu.VMEM((n_out,) + block, BF16),
            pltpu.VMEM((n_line, CASES, shift_factors.shape[1]), BF16),
            dma((2, n_line)),
            dma((2, n_line)),
            dma((2, n_out)),
            dma((2, n_out)),
            dma((2, n_line)),
        ],
        compiler_params=pltpu.CompilerParams(
            collective_id=1, has_side_effects=True, vmem_limit_bytes=40 * 2**20
        ),
        name="grads",
    )(direct, reverse, outage_line.reshape(1, n_k), shift_factors)


def shards(
    n_line, n_out, injections, shift_factors, outage_factors, limits, outage_line, tile_list, tile_count
):
    lf, ff = flows(n_line, n_out, injections, shift_factors, outage_line)
    direct, reverse = terms(n_line, n_out, tile_list, tile_count, outage_factors, lf, limits, ff)
    return grads(n_line, n_out, direct, reverse, outage_line, shift_factors)


def solution(mesh):
    placed = (
        P(None, "out"),
        P("line", "out"),
        P("out", "line"),
        P("line"),
        P("out"),
        P("out", None),
        P("out"),
    )
    return jax.shard_map(
        functools.partial(shards, mesh.shape["line"], mesh.shape["out"]),
        mesh=mesh,
        in_specs=placed,
        out_specs=P(None, "out"),
        check_vma=False,
    )
```

```python
import functools

import jax
import jax.numpy as jnp
from jax import lax
from jax.experimental import pallas as pl
from jax.experimental.pallas import tpu as pltpu
from jax.sharding import PartitionSpec as P

CASES = 32
NO = 16384
TILE = 64
GROUP = 4
LB = 128
F32 = jnp.float32
BF16 = jnp.bfloat16
MESH = pl.DeviceIdType.MESH
VMEM = pl.BlockSpec(memory_space=pltpu.VMEM)
SMEM = pl.BlockSpec(memory_space=pltpu.SMEM)
HBM = pl.BlockSpec(memory_space=pltpu.HBM)


LINE_STEPS = [(1, 2), (1, 1), (1, 3), (0, 2), (1, 0), (0, 1), (0, 3)]
OUT_STEPS = [(x, y, c) for x, y in [(1, 2), (1, 1), (1, 3), (0, 2), (1, 0), (0, 1), (0, 3)] for c in (1, 0)]
OUT_STEPS += [(0, 0, 1)]
STEPS = {"line": LINE_STEPS, "out": OUT_STEPS}


def partner(axis, i):
    me = lax.axis_index(axis)
    if axis == "line":
        dx, dz = LINE_STEPS[i]
        return lax.rem(me // 4 + dx, 2) * 4 + lax.rem(lax.rem(me, 4) + dz, 4)
    dx, dy, dc = OUT_STEPS[i]
    x, y, c = me // 8, lax.rem(me // 2, 4), lax.rem(me, 2)
    return lax.rem(x + dx, 2) * 8 + lax.rem(y + dy, 4) * 2 + lax.rem(c + dc, 2)


def peer(axis, i):
    if axis == "out":
        return (lax.axis_index("line"), partner(axis, i))
    return (partner(axis, i), lax.axis_index("out"))


def greet():
    barrier = pltpu.get_barrier_semaphore()
    for axis in ("out", "line"):
        for i in range(len(STEPS[axis])):
            pl.semaphore_signal(barrier, inc=1, device_id=peer(axis, i), device_id_type=MESH)
    return barrier


def send(src, dst, sems, i, axis):
    copy = pltpu.make_async_remote_copy(
        src_ref=src,
        dst_ref=dst,
        send_sem=sems.at[0, i],
        recv_sem=sems.at[1, i],
        device_id=peer(axis, i),
        device_id_type=MESH,
    )
    copy.start()
    return copy


def split3(x):
    hi = x.astype(BF16)
    rest = x - hi.astype(F32)
    mid = rest.astype(BF16)
    low = (rest - mid.astype(F32)).astype(BF16)
    return jnp.concatenate([hi, mid, low], axis=0)


def send_parts(parts, recv, sems, axis, fill=None):
    copies = []
    for i in range(len(STEPS[axis])):
        d = partner(axis, i)
        if fill is not None:
            fill(d)
        copies.append(send(parts.at[d], recv.at[i], sems, i, axis))
    if fill is not None:
        fill(lax.axis_index(axis))
    return copies


def sum_parts(parts, recv, copies, axis):
    total = parts[lax.axis_index(axis)]
    for i in reversed(range(len(copies))):
        copies[i].wait_recv()
        total = total + recv[i]
    return total


def finish(copies):
    for copy in copies:
        copy.wait_send()


def spread(slots, sems, axis):
    me = lax.axis_index(axis)
    copies = [send(slots.at[me], slots.at[me], sems, i, axis) for i in range(len(STEPS[axis]))]
    for copy in copies:
        copy.wait_recv()
    return copies


def hot_table(hot, line_ref, n_out, n_k):
    local = line_ref[...] - lax.axis_index("line") * (n_out * LB)

    def hot_rows(r, _):
        base = pl.multiple_of(r * LB, LB)
        ids = lax.broadcasted_iota(jnp.int32, (LB, n_k), 0) + base
        hot[pl.ds(base, LB), :] = (ids == local).astype(F32).astype(BF16)
        return 0

    lax.fori_loop(0, n_out, hot_rows, 0)


def flows_kernel(
    n_line, n_out, inj_ref, sf_ref, line_ref, lf_ref, ff_ref,
    inj, sf, line, parts, recv_o, slots_o, hot, picked, recv_l, slots_l,
    s_in, s_ro, s_go, s_rl, s_gl,
):
    loads = [
        pltpu.make_async_copy(src, dst, s_in.at[i])
        for i, (src, dst) in enumerate([(inj_ref, inj), (sf_ref, sf), (line_ref, line)])
    ]
    for load in loads:
        load.start()
    barrier = greet()
    for load in loads:
        load.wait()
    for d in range(n_out):
        parts[d] = lax.dot_general(
            inj[...], sf[d * LB : (d + 1) * LB, :], (((1,), (1,)), ((), ())), preferred_element_type=F32
        )
    pl.semaphore_wait(barrier, n_out + n_line - 2)
    sent = send_parts(parts, recv_o, s_ro, "out")
    hot_table(hot, line, n_out, n_line * LB)
    slots_o[lax.axis_index("out")] = sum_parts(parts, recv_o, sent, "out")
    sent += spread(slots_o, s_go, "out")
    wide = jnp.concatenate([slots_o[i] for i in range(n_out)], axis=1)
    got = jnp.dot(split3(wide), hot[...], preferred_element_type=F32)
    got = got[:CASES] + got[CASES : 2 * CASES] + got[2 * CASES :]
    for i in range(n_line):
        picked[i] = got[:, i * LB : (i + 1) * LB]
    sent += send_parts(picked, recv_l, s_rl, "line")
    lf_ref[...] = slots_o[...]
    slots_l[lax.axis_index("line")] = sum_parts(picked, recv_l, sent[-len(LINE_STEPS) :], "line")
    sent += spread(slots_l, s_gl, "line")
    ff_ref[...] = slots_l[...]
    finish(sent)


def flows(n_line, n_out, injections, shift_factors, outage_line):
    n_k = n_line * LB
    block = (CASES, LB)
    dma = pltpu.SemaphoreType.DMA
    line_row = outage_line.reshape(1, n_k)
    return pl.pallas_call(
        functools.partial(flows_kernel, n_line, n_out),
        in_specs=[HBM, HBM, HBM],
        out_specs=[VMEM, VMEM],
        out_shape=[
            jax.ShapeDtypeStruct((n_out,) + block, F32),
            jax.ShapeDtypeStruct((n_line,) + block, F32),
        ],
        scratch_shapes=[
            pltpu.VMEM(injections.shape, BF16),
            pltpu.VMEM(shift_factors.shape, BF16),
            pltpu.VMEM(line_row.shape, jnp.int32),
            pltpu.VMEM((n_out,) + block, F32),
            pltpu.VMEM((n_out,) + block, F32),
            pltpu.VMEM((n_out,) + block, F32),
            pltpu.VMEM((n_out * LB, n_k), BF16),
            pltpu.VMEM((n_line,) + block, F32),
            pltpu.VMEM((n_line,) + block, F32),
            pltpu.VMEM((n_line,) + block, F32),
            dma((3,)),
            dma((2, n_out)),
            dma((2, n_out)),
            dma((2, n_line)),
            dma((2, n_line)),
        ],
        compiler_params=pltpu.CompilerParams(
            collective_id=0, has_side_effects=True, vmem_limit_bytes=63 * 2**20
        ),
        name="flows",
    )(injections, shift_factors, line_row)


def terms_kernel(
    n_line, n_out, list_ref, count_ref, of_ref, lf_ref, lim_ref, ff_ref, dir_ref, rev_ref,
    wide_of, low, high, fall, dsum, qsum, turned, rsum,
):
    for t in range(n_out):
        cols = pl.ds(t * LB, LB)
        lim = lim_ref[:, cols]
        flow = lf_ref[t]
        for c in range(CASES):
            low[c, :, cols] = jnp.broadcast_to(-lim - flow[c : c + 1], (8, LB))
            high[c, :, cols] = jnp.broadcast_to(lim - flow[c : c + 1], (8, LB))
    for b in range(n_line):
        turned[b * LB : (b + 1) * LB, 0:CASES] = ff_ref[b].T
    dsum[...] = jnp.zeros_like(dsum)
    qsum[...] = jnp.zeros_like(qsum)
    rsum[...] = jnp.zeros_like(rsum)
    n_sub = TILE // 8
    lanes = lax.broadcasted_iota(jnp.int32, (8, LB), 1)

    def tile_step(step, _):
        tile = list_ref[0, step]
        k0 = pl.multiple_of(tile * TILE, TILE)
        narrow = of_ref[pl.ds(k0, TILE), :]
        wide_of[...] = narrow.astype(F32)
        pair = ff_ref[tile // 2]
        half = lax.rem(tile, 2) == 0
        mine = jnp.where(half, pair[:, :TILE], pair[:, TILE:])
        prod = jnp.dot(split3(mine), narrow, preferred_element_type=F32)
        qsum[...] += prod[:CASES] + prod[CASES : 2 * CASES] + prod[2 * CASES :]
        square = jnp.zeros((TILE, LB), F32)
        for t in range(n_out):
            w = wide_of[:, t * LB : (t + 1) * LB]
            square = square + w * w
        for c in range(CASES):
            fall[c] = jnp.broadcast_to(turned[pl.ds(k0, TILE), c : c + 1], (TILE, LB))

        def reduce_rows(c, sums):
            return tuple(
                jnp.where(lanes == c, jnp.sum(fall[jnp.maximum(c, 0), 8 * i : 8 * i + 8, :], axis=1, keepdims=True), sums[i])
                for i in range(n_sub)
            )

        def case_step(c):
            ffs = [fall[c, 8 * i : 8 * i + 8, :] for i in range(n_sub)]
            acc = [ffs[i] * square[8 * i : 8 * i + 8] for i in range(n_sub)]
            for t in range(n_out):
                cols = pl.ds(t * LB, LB)
                lo = low[c, :, cols]
                hi = high[c, :, cols]
                qs = []
                for i in range(n_sub):
                    o = wide_of[8 * i : 8 * i + 8, t * LB : (t + 1) * LB]
                    q = jnp.minimum(jnp.maximum(ffs[i] * o, lo), hi)
                    acc[i] = acc[i] - q * o
                    qs.append(q)
                while len(qs) > 1:
                    qs = [qs[i] + qs[i + 1] for i in range(0, len(qs), 2)]
                dsum[c, :, cols] += qs[0]
            for i in range(n_sub):
                fall[c, 8 * i : 8 * i + 8, :] = acc[i]

        def group_step(g, sums):
            for e in range(GROUP):
                sums = reduce_rows(g * GROUP - GROUP + e, sums)
            for e in range(GROUP):
                case_step(g * GROUP + e)
            return sums

        zero = jnp.zeros((8, LB), F32)
        sums = lax.fori_loop(0, CASES // GROUP, group_step, (zero,) * n_sub)
        for e in range(GROUP):
            sums = reduce_rows(CASES - GROUP + e, sums)
        for i in range(n_sub):
            rsum[pl.ds(k0 + 8 * i, 8), :] = sums[i]
        return 0

    lax.fori_loop(0, count_ref[0], tile_step, 0)
    for t in range(n_out):
        cols = slice(t * LB, (t + 1) * LB)
        dir_ref[t] = qsum[:, cols] - jnp.sum(dsum[:, :, cols], axis=1)
    for b in range(n_line):
        rev_ref[b] = rsum[b * LB : (b + 1) * LB, :].T[:CASES]


def terms(n_line, n_out, tile_list, tile_count, outage_factors, lf, limits, ff):
    n_l = n_out * LB
    n_k = n_line * LB
    block = (CASES, LB)
    return pl.pallas_call(
        functools.partial(terms_kernel, n_line, n_out),
        in_specs=[SMEM, SMEM, VMEM, VMEM, VMEM, VMEM],
        out_specs=[VMEM, VMEM],
        out_shape=[
            jax.ShapeDtypeStruct((n_out,) + block, F32),
            jax.ShapeDtypeStruct((n_line,) + block, F32),
        ],
        scratch_shapes=[
            pltpu.VMEM((TILE, n_l), F32),
            pltpu.VMEM((CASES, 8, n_l), F32),
            pltpu.VMEM((CASES, 8, n_l), F32),
            pltpu.VMEM((CASES, TILE, LB), F32),
            pltpu.VMEM((CASES, 8, n_l), F32),
            pltpu.VMEM((CASES, n_l), F32),
            pltpu.VMEM((n_k, LB), F32),
            pltpu.VMEM((n_k, LB), F32),
        ],
        compiler_params=pltpu.CompilerParams(vmem_limit_bytes=63 * 2**20),
        name="terms",
    )(tile_list, tile_count, outage_factors, lf, limits.reshape(1, n_l), ff)


def grads_kernel(
    n_line, n_out, dir_ref, rev_ref, line_ref, sf_ref, out_ref,
    line, sf, recv_r, slots_r, hot, parts, recv_o, slots_o, slots_f,
    s_in, s_rr, s_gr, s_ro, s_go, s_gf,
):
    loads = [
        pltpu.make_async_copy(src, dst, s_in.at[i])
        for i, (src, dst) in enumerate([(line_ref, line), (sf_ref, sf)])
    ]
    barrier = greet()
    for load in loads:
        load.start()
    pl.semaphore_wait(barrier, n_out + n_line - 2)
    sent = send_parts(rev_ref, recv_r, s_rr, "line")
    loads[0].wait()
    hot_table(hot, line, n_out, n_line * LB)
    slots_r[lax.axis_index("line")] = sum_parts(rev_ref, recv_r, sent, "line")
    sent += spread(slots_r, s_gr, "line")
    three = split3(jnp.concatenate([slots_r[i] for i in range(n_line)], axis=1))

    def fill(d):
        table = hot[pl.ds(pl.multiple_of(d * LB, LB), LB), :]
        got = lax.dot_general(three, table, (((1,), (1,)), ((), ())), preferred_element_type=F32)
        parts[d] = dir_ref[d] + (got[:CASES] + got[CASES : 2 * CASES] + got[2 * CASES :])

    scattered = send_parts(parts, recv_o, s_ro, "out", fill)
    grad = sum_parts(parts, recv_o, scattered, "out")
    slots_o[lax.axis_index("out")] = (grad * (2.0 / NO)).astype(BF16)
    sent += scattered + spread(slots_o, s_go, "out")
    rounded = jnp.concatenate([slots_o[i] for i in range(n_out)], axis=1)
    loads[1].wait()
    partial = jnp.dot(rounded, sf[...], preferred_element_type=F32)
    slots_f[lax.axis_index("line")] = partial.astype(BF16)
    sent += spread(slots_f, s_gf, "line")
    result = slots_f[0].astype(F32)
    for i in range(1, n_line):
        result = result + slots_f[i].astype(F32)
    out_ref[...] = result
    finish(sent)


def grads(n_line, n_out, direct, reverse, outage_line, shift_factors):
    n_k = n_line * LB
    block = (CASES, LB)
    dma = pltpu.SemaphoreType.DMA
    return pl.pallas_call(
        functools.partial(grads_kernel, n_line, n_out),
        in_specs=[VMEM, VMEM, HBM, HBM],
        out_specs=VMEM,
        out_shape=jax.ShapeDtypeStruct((CASES, shift_factors.shape[1]), F32),
        scratch_shapes=[
            pltpu.VMEM((1, n_k), jnp.int32),
            pltpu.VMEM(shift_factors.shape, BF16),
            pltpu.VMEM((n_line,) + block, F32),
            pltpu.VMEM((n_line,) + block, F32),
            pltpu.VMEM((n_out * LB, n_k), BF16),
            pltpu.VMEM((n_out,) + block, F32),
            pltpu.VMEM((n_out,) + block, F32),
            pltpu.VMEM((n_out,) + block, BF16),
            pltpu.VMEM((n_line, CASES, shift_factors.shape[1]), BF16),
            dma((2,)),
            dma((2, n_line)),
            dma((2, n_line)),
            dma((2, n_out)),
            dma((2, n_out)),
            dma((2, n_line)),
        ],
        compiler_params=pltpu.CompilerParams(
            collective_id=1, has_side_effects=True, vmem_limit_bytes=63 * 2**20
        ),
        name="grads",
    )(direct, reverse, outage_line.reshape(1, n_k), shift_factors)


def shards(
    n_line, n_out, injections, shift_factors, outage_factors, limits, outage_line, tile_list, tile_count
):
    lf, ff = flows(n_line, n_out, injections, shift_factors, outage_line)
    direct, reverse = terms(n_line, n_out, tile_list, tile_count, outage_factors, lf, limits, ff)
    return grads(n_line, n_out, direct, reverse, outage_line, shift_factors)


def solution(mesh):
    placed = (
        P(None, "out"),
        P("line", "out"),
        P("out", "line"),
        P("line"),
        P("out"),
        P("out", None),
        P("out"),
    )
    return jax.shard_map(
        functools.partial(shards, mesh.shape["line"], mesh.shape["out"]),
        mesh=mesh,
        in_specs=placed,
        out_specs=P(None, "out"),
        check_vma=False,
    )
```

```python
import functools

import jax
import jax.numpy as jnp
from jax import lax
from jax.experimental import pallas as pl
from jax.experimental.pallas import tpu as pltpu
from jax.sharding import PartitionSpec as P

CASES = 32
NO = 16384
TILE = 64
GROUP = 4
LB = 128
F32 = jnp.float32
BF16 = jnp.bfloat16
MESH = pl.DeviceIdType.MESH
VMEM = pl.BlockSpec(memory_space=pltpu.VMEM)
HBM = pl.BlockSpec(memory_space=pltpu.HBM)


LINE_STEPS = [(1, 2), (1, 1), (1, 3), (0, 2), (1, 0), (0, 1), (0, 3)]
OUT_STEPS = [(x, y, c) for x, y in [(1, 2), (1, 1), (1, 3), (0, 2), (1, 0), (0, 1), (0, 3)] for c in (1, 0)]
OUT_STEPS += [(0, 0, 1)]
STEPS = {"line": LINE_STEPS, "out": OUT_STEPS}


def partner(axis, i):
    me = lax.axis_index(axis)
    if axis == "line":
        dx, dz = LINE_STEPS[i]
        return lax.rem(me // 4 + dx, 2) * 4 + lax.rem(lax.rem(me, 4) + dz, 4)
    dx, dy, dc = OUT_STEPS[i]
    x, y, c = me // 8, lax.rem(me // 2, 4), lax.rem(me, 2)
    return lax.rem(x + dx, 2) * 8 + lax.rem(y + dy, 4) * 2 + lax.rem(c + dc, 2)


def peer(axis, i):
    if axis == "out":
        return (lax.axis_index("line"), partner(axis, i))
    return (partner(axis, i), lax.axis_index("out"))


def greet():
    barrier = pltpu.get_barrier_semaphore()
    for axis in ("out", "line"):
        for i in range(len(STEPS[axis])):
            pl.semaphore_signal(barrier, inc=1, device_id=peer(axis, i), device_id_type=MESH)
    return barrier


def send(src, dst, sems, i, axis):
    copy = pltpu.make_async_remote_copy(
        src_ref=src,
        dst_ref=dst,
        send_sem=sems.at[0, i],
        recv_sem=sems.at[1, i],
        device_id=peer(axis, i),
        device_id_type=MESH,
    )
    copy.start()
    return copy


def split3(x):
    hi = x.astype(BF16)
    rest = x - hi.astype(F32)
    mid = rest.astype(BF16)
    low = (rest - mid.astype(F32)).astype(BF16)
    return jnp.concatenate([hi, mid, low], axis=0)


def send_parts(parts, recv, sems, axis, fill=None):
    copies = []
    for i in range(len(STEPS[axis])):
        d = partner(axis, i)
        if fill is not None:
            fill(d)
        copies.append(send(parts.at[d], recv.at[i], sems, i, axis))
    if fill is not None:
        fill(lax.axis_index(axis))
    return copies


def sum_parts(parts, recv, copies, axis):
    total = parts[lax.axis_index(axis)]
    for i in reversed(range(len(copies))):
        copies[i].wait_recv()
        total = total + recv[i]
    return total


def finish(copies):
    for copy in copies:
        copy.wait_send()


def spread(slots, sems, axis, meanwhile=None):
    me = lax.axis_index(axis)
    copies = [send(slots.at[me], slots.at[me], sems, i, axis) for i in range(len(STEPS[axis]))]
    if meanwhile is not None:
        meanwhile()
    for copy in copies:
        copy.wait_recv()
    return copies


def hot_table(hot, line_ref, n_out, n_k):
    local = line_ref[...] - lax.axis_index("line") * (n_out * LB)

    def hot_rows(r, _):
        base = pl.multiple_of(r * LB, LB)
        ids = lax.broadcasted_iota(jnp.int32, (LB, n_k), 0) + base
        hot[pl.ds(base, LB), :] = (ids == local).astype(F32).astype(BF16)
        return 0

    lax.fori_loop(0, n_out, hot_rows, 0)


def add3(x):
    return x[:CASES] + x[CASES : 2 * CASES] + x[2 * CASES :]


def gradient_kernel(
    n_line, n_out, inj_hbm, sf_hbm, of_hbm, lim_hbm, line_hbm, list_ref, count_ref, out_ref,
    inj, sf, of, lim, line, parts, recv_o, slots_o, hot, picked, recv_l, slots_l,
    wide_of, square, low, high, fall, dsum, qsum, turned, rsum, act,
    rev, recv_r, slots_r, terms, recv_t, slots_g, slots_f,
    s_in, s_ro, s_go, s_rl, s_gl, s_rr, s_gr, s_rt, s_gg, s_gf,
):
    n_k = n_line * LB
    n_tiles = n_k // TILE
    n_sub = TILE // 8
    me_line = lax.axis_index("line")
    me_out = lax.axis_index("out")
    loads = [
        pltpu.make_async_copy(src, dst, s_in.at[i])
        for i, (src, dst) in enumerate(
            [(inj_hbm, inj), (sf_hbm, sf), (line_hbm, line), (lim_hbm, lim), (of_hbm, of)]
        )
    ]
    for load in loads:
        load.start()
    barrier = greet()

    def widen(first, last):
        def one(tile, _):
            rows = pl.ds(pl.multiple_of(tile * TILE, TILE), TILE)
            total = jnp.zeros((TILE, LB), F32)
            for t in range(n_out):
                w = of[rows, t * LB : (t + 1) * LB].astype(F32)
                wide_of[rows, t * LB : (t + 1) * LB] = w
                total = total + w * w
            square[rows, :] = total
            return 0

        lax.fori_loop(first, last, one, 0)

    loads[0].wait()
    loads[1].wait()
    for d in range(n_out):
        parts[d] = lax.dot_general(
            inj[...], sf[d * LB : (d + 1) * LB, :], (((1,), (1,)), ((), ())), preferred_element_type=F32
        )
    pl.semaphore_wait(barrier, n_out + n_line - 2)
    sent = send_parts(parts, recv_o, s_ro, "out")
    for load in loads[2:]:
        load.wait()
    hot_table(hot, line, n_out, n_k)
    widen(0, n_tiles // 2)
    slots_o[me_out] = sum_parts(parts, recv_o, sent, "out")
    sent += spread(slots_o, s_go, "out", lambda: widen(n_tiles // 2, n_tiles))
    flow = jnp.concatenate([slots_o[i] for i in range(n_out)], axis=1)
    got = add3(jnp.dot(split3(flow), hot[...], preferred_element_type=F32))
    for i in range(n_line):
        picked[i] = got[:, i * LB : (i + 1) * LB]
    picks = send_parts(picked, recv_l, s_rl, "line")
    sent += picks
    for t in range(n_out):
        cols = slice(t * LB, (t + 1) * LB)
        for c in range(CASES):
            low[c, :, cols] = jnp.broadcast_to(-lim[:, cols] - slots_o[t, c : c + 1, :], (8, LB))
            high[c, :, cols] = jnp.broadcast_to(lim[:, cols] - slots_o[t, c : c + 1, :], (8, LB))
    slots_l[me_line] = sum_parts(picked, recv_l, picks, "line")

    def clear():
        dsum[...] = jnp.zeros_like(dsum)
        qsum[...] = jnp.zeros_like(qsum)
        ids = lax.broadcasted_iota(jnp.int32, (n_tiles, n_tiles), 0)
        place = lax.broadcasted_iota(jnp.int32, (n_tiles, n_tiles), 1)
        listed = (list_ref[...] == ids) & (place < count_ref[...])
        flags = jnp.sum(jnp.where(listed, 1.0, 0.0), axis=1, keepdims=True)
        act[...] = jnp.broadcast_to(flags, (n_tiles, LB))

    sent += spread(slots_l, s_gl, "line", clear)
    for b in range(n_line):
        turned[b * LB : (b + 1) * LB, 0:CASES] = slots_l[b].T
    lanes = lax.broadcasted_iota(jnp.int32, (TILE, LB), 1)

    def tile_step(tile, _):
        k0 = pl.multiple_of(tile * TILE, TILE)
        rows = pl.ds(k0, TILE)
        on = act[pl.ds(tile, 1), :]
        pair = slots_l[tile // 2]
        mine = jnp.where(lax.rem(tile, 2) == 0, pair[:, :TILE], pair[:, TILE:]) * on[:, :TILE]
        qsum[...] += add3(jnp.dot(split3(mine), of[rows, :], preferred_element_type=F32))
        for c in range(CASES):
            fall[c] = jnp.broadcast_to(turned[rows, c : c + 1], (TILE, LB))

        def reduce_rows(c, sums):
            return jnp.where(lanes == c, jnp.sum(fall[jnp.maximum(c, 0)], axis=1, keepdims=True), sums)

        def case_step(c):
            ffs = fall[c]
            acc = ffs * square[rows, :]
            for t in range(n_out):
                cols = slice(t * LB, (t + 1) * LB)
                lo = jnp.concatenate([low[c, :, cols]] * n_sub, axis=0)
                hi = jnp.concatenate([high[c, :, cols]] * n_sub, axis=0)
                o = wide_of[rows, cols]
                q = jnp.minimum(jnp.maximum(ffs * o, lo), hi)
                acc = acc - q * o
                size = TILE // 2
                while size >= 8:
                    q = q[:size] + q[size:]
                    size //= 2
                dsum[c, :, cols] += q * on
            fall[c] = acc

        def group_step(g, sums):
            for e in range(GROUP):
                sums = reduce_rows(g * GROUP - GROUP + e, sums)
            for e in range(GROUP):
                case_step(g * GROUP + e)
            return sums

        sums = lax.fori_loop(0, CASES // GROUP, group_step, jnp.zeros((TILE, LB), F32))
        for e in range(GROUP):
            sums = reduce_rows(CASES - GROUP + e, sums)
        rsum[rows, :] = sums * on
        return 0

    lax.fori_loop(0, n_tiles, tile_step, 0)

    for b in range(n_line):
        rev[b] = rsum[b * LB : (b + 1) * LB, :].T[:CASES]
    turns = send_parts(rev, recv_r, s_rr, "line")
    sent += turns
    for t in range(n_out):
        cols = slice(t * LB, (t + 1) * LB)
        terms[t] = qsum[:, cols] - jnp.sum(dsum[:, :, cols], axis=1)
    slots_r[me_line] = sum_parts(rev, recv_r, turns, "line")
    sent += spread(slots_r, s_gr, "line")
    three = split3(jnp.concatenate([slots_r[i] for i in range(n_line)], axis=1))

    def fill(d):
        table = hot[pl.ds(pl.multiple_of(d * LB, LB), LB), :]
        terms[d] += add3(
            lax.dot_general(three, table, (((1,), (1,)), ((), ())), preferred_element_type=F32)
        )

    scattered = send_parts(terms, recv_t, s_rt, "out", fill)
    grad = sum_parts(terms, recv_t, scattered, "out")
    slots_g[me_out] = (grad * (2.0 / NO)).astype(BF16)
    sent += scattered + spread(slots_g, s_gg, "out")
    rounded = jnp.concatenate([slots_g[i] for i in range(n_out)], axis=1)
    partial = jnp.dot(rounded, sf[...], preferred_element_type=F32)
    slots_f[me_line] = partial.astype(BF16)
    sent += spread(slots_f, s_gf, "line")
    result = slots_f[0].astype(F32)
    for i in range(1, n_line):
        result = result + slots_f[i].astype(F32)
    out_ref[...] = result
    finish(sent)


def shards(
    n_line, n_out, injections, shift_factors, outage_factors, limits, outage_line, tile_list, tile_count
):
    n_k = n_line * LB
    n_l = n_out * LB
    block = (CASES, LB)
    dma = pltpu.SemaphoreType.DMA
    line_row = outage_line.reshape(1, n_k)
    limit_row = limits.reshape(1, n_l)
    per_line = pltpu.VMEM((n_line,) + block, F32)
    per_out = pltpu.VMEM((n_out,) + block, F32)
    return pl.pallas_call(
        functools.partial(gradient_kernel, n_line, n_out),
        in_specs=[HBM] * 5 + [VMEM] * 2,
        out_specs=VMEM,
        out_shape=jax.ShapeDtypeStruct((CASES, shift_factors.shape[1]), F32),
        scratch_shapes=[
            pltpu.VMEM(injections.shape, BF16),
            pltpu.VMEM(shift_factors.shape, BF16),
            pltpu.VMEM(outage_factors.shape, BF16),
            pltpu.VMEM(limit_row.shape, F32),
            pltpu.VMEM(line_row.shape, jnp.int32),
            per_out,
            per_out,
            per_out,
            pltpu.VMEM((n_l, n_k), BF16),
            per_line,
            per_line,
            per_line,
            pltpu.VMEM((n_k, n_l), F32),
            pltpu.VMEM((n_k, LB), F32),
            pltpu.VMEM((CASES, 8, n_l), F32),
            pltpu.VMEM((CASES, 8, n_l), F32),
            pltpu.VMEM((CASES, TILE, LB), F32),
            pltpu.VMEM((CASES, 8, n_l), F32),
            pltpu.VMEM((CASES, n_l), F32),
            pltpu.VMEM((n_k, LB), F32),
            pltpu.VMEM((n_k, LB), F32),
            pltpu.VMEM((n_k // TILE, LB), F32),
            per_line,
            per_line,
            per_line,
            per_out,
            per_out,
            pltpu.VMEM((n_out,) + block, BF16),
            pltpu.VMEM((n_line, CASES, shift_factors.shape[1]), BF16),
            dma((5,)),
            dma((2, n_out)),
            dma((2, n_out)),
            dma((2, n_line)),
            dma((2, n_line)),
            dma((2, n_line)),
            dma((2, n_line)),
            dma((2, n_out)),
            dma((2, n_out)),
            dma((2, n_line)),
        ],
        compiler_params=pltpu.CompilerParams(
            collective_id=0, has_side_effects=True, vmem_limit_bytes=63 * 2**20
        ),
        name="gradient",
    )(injections, shift_factors, outage_factors, limit_row, line_row, tile_list, tile_count.reshape(1, 1))


def solution(mesh):
    placed = (
        P(None, "out"),
        P("line", "out"),
        P("out", "line"),
        P("line"),
        P("out"),
        P("out", None),
        P("out"),
    )
    return jax.shard_map(
        functools.partial(shards, mesh.shape["line"], mesh.shape["out"]),
        mesh=mesh,
        in_specs=placed,
        out_specs=P(None, "out"),
        check_vma=False,
    )
```

```python
import functools

import jax
import jax.numpy as jnp
from jax import lax
from jax.experimental import pallas as pl
from jax.experimental.pallas import tpu as pltpu
from jax.sharding import PartitionSpec as P

CASES = 32
NO = 16384
TILE = 64
GROUP = 4
LB = 128
F32 = jnp.float32
BF16 = jnp.bfloat16
MESH = pl.DeviceIdType.MESH
VMEM = pl.BlockSpec(memory_space=pltpu.VMEM)
HBM = pl.BlockSpec(memory_space=pltpu.HBM)


LINE_STEPS = [(1, 2), (1, 1), (1, 3), (0, 2), (1, 0), (0, 1), (0, 3)]
OUT_STEPS = [(x, y, c) for x, y in [(1, 2), (1, 1), (1, 3), (0, 2), (1, 0), (0, 1), (0, 3)] for c in (1, 0)]
OUT_STEPS += [(0, 0, 1)]
FALL_PIECES = [(0, 1), (1, 1), (2, 6)]
TERM_PIECES = [(0, 4), (4, 3), (7, 1)]
STEPS = {"line": LINE_STEPS, "out": OUT_STEPS}


def partner(axis, i):
    me = lax.axis_index(axis)
    if axis == "line":
        dx, dz = LINE_STEPS[i]
        return lax.rem(me // 4 + dx, 2) * 4 + lax.rem(lax.rem(me, 4) + dz, 4)
    dx, dy, dc = OUT_STEPS[i]
    x, y, c = me // 8, lax.rem(me // 2, 4), lax.rem(me, 2)
    return lax.rem(x + dx, 2) * 8 + lax.rem(y + dy, 4) * 2 + lax.rem(c + dc, 2)


def peer(axis, i):
    if axis == "out":
        return (lax.axis_index("line"), partner(axis, i))
    return (partner(axis, i), lax.axis_index("out"))


def greet():
    barrier = pltpu.get_barrier_semaphore()
    for axis in ("out", "line"):
        for i in range(len(STEPS[axis])):
            pl.semaphore_signal(barrier, inc=1, device_id=peer(axis, i), device_id_type=MESH)
    return barrier


def send(src, dst, sems, i, axis):
    copy = pltpu.make_async_remote_copy(
        src_ref=src,
        dst_ref=dst,
        send_sem=sems.at[0, i],
        recv_sem=sems.at[1, i],
        device_id=peer(axis, i),
        device_id_type=MESH,
    )
    copy.start()
    return copy


def split3(x):
    hi = x.astype(BF16)
    rest = x - hi.astype(F32)
    mid = rest.astype(BF16)
    low = (rest - mid.astype(F32)).astype(BF16)
    return jnp.concatenate([hi, mid, low], axis=0)


def send_parts(parts, recv, sems, axis, fill=None):
    copies = []
    for i in range(len(STEPS[axis])):
        d = partner(axis, i)
        if fill is not None:
            fill(d)
        copies.append(send(parts.at[d], recv.at[i], sems, i, axis))
    if fill is not None:
        fill(lax.axis_index(axis))
    return copies


def sum_parts(parts, recv, copies, axis):
    total = parts[lax.axis_index(axis)]
    for i in reversed(range(len(copies))):
        copies[i].wait_recv()
        total = total + recv[i]
    return total


def finish(copies):
    for copy in copies:
        copy.wait_send()


def spread(slots, sems, axis, meanwhile=None):
    me = lax.axis_index(axis)
    copies = [send(slots.at[me], slots.at[me], sems, i, axis) for i in range(len(STEPS[axis]))]
    if meanwhile is not None:
        meanwhile()
    for copy in copies:
        copy.wait_recv()
    return copies


def hot_table(hot, line_ref, n_out, n_k):
    local = line_ref[...] - lax.axis_index("line") * (n_out * LB)

    def hot_rows(r, _):
        base = pl.multiple_of(r * LB, LB)
        ids = lax.broadcasted_iota(jnp.int32, (LB, n_k), 0) + base
        hot[pl.ds(base, LB), :] = (ids == local).astype(F32).astype(BF16)
        return 0

    lax.fori_loop(0, n_out, hot_rows, 0)


def message(src, dst, sems, m, i, piece):
    return pltpu.make_async_remote_copy(
        src_ref=src.at[pl.ds(*piece)],
        dst_ref=dst.at[i, pl.ds(*piece)],
        send_sem=sems.at[0, m, i],
        recv_sem=sems.at[1, m, i],
        device_id=peer("line", i),
        device_id_type=MESH,
    )


def add3(x):
    return x[:CASES] + x[CASES : 2 * CASES] + x[2 * CASES :]


def gradient_kernel(
    n_line, n_out, inj_hbm, sf_hbm, of_hbm, lim_hbm, line_hbm, list_ref, count_ref, out_ref,
    inj, sf, of, lim, line, parts, recv_o, slots_o, hot, picked, recv_l, slots_l,
    wide_of, square, low, high, fall, dsum, qsum, turned, rsum, act,
    rev, recv_r, terms, recv_t, slots_g, slots_f,
    s_in, s_ro, s_go, s_rl, s_rr, s_rt, s_gg, s_gf,
):
    n_k = n_line * LB
    n_tiles = n_k // TILE
    n_sub = TILE // 8
    me_line = lax.axis_index("line")
    me_out = lax.axis_index("out")
    loads = [
        pltpu.make_async_copy(src, dst, s_in.at[i])
        for i, (src, dst) in enumerate(
            [(inj_hbm, inj), (sf_hbm, sf), (line_hbm, line), (lim_hbm, lim), (of_hbm, of)]
        )
    ]
    for load in loads:
        load.start()
    barrier = greet()

    def widen(first, last):
        def one(tile, _):
            rows = pl.ds(pl.multiple_of(tile * TILE, TILE), TILE)
            total = jnp.zeros((TILE, LB), F32)
            for t in range(n_out):
                w = of[rows, t * LB : (t + 1) * LB].astype(F32)
                wide_of[rows, t * LB : (t + 1) * LB] = w
                total = total + w * w
            square[rows, :] = total
            return 0

        lax.fori_loop(first, last, one, 0)

    loads[0].wait()
    loads[1].wait()
    for d in range(n_out):
        parts[d] = lax.dot_general(
            inj[...], sf[d * LB : (d + 1) * LB, :], (((1,), (1,)), ((), ())), preferred_element_type=F32
        )
    pl.semaphore_wait(barrier, n_out + n_line - 2)
    sent = send_parts(parts, recv_o, s_ro, "out")
    for load in loads[2:]:
        load.wait()
    hot_table(hot, line, n_out, n_k)
    widen(0, n_tiles // 2)
    slots_o[me_out] = sum_parts(parts, recv_o, sent, "out")
    sent += spread(slots_o, s_go, "out", lambda: widen(n_tiles // 2, n_tiles))
    flow = jnp.concatenate([slots_o[i] for i in range(n_out)], axis=1)
    got = add3(jnp.dot(split3(flow), hot[...], preferred_element_type=F32))
    for i in range(n_line):
        picked[i] = got[:, i * LB : (i + 1) * LB]
    falls = [[message(picked, recv_l, s_rl, m, i, FALL_PIECES[m]) for i in range(n_line - 1)] for m in range(3)]
    for piece in falls:
        for copy in piece:
            copy.start()
    for t in range(n_out):
        cols = slice(t * LB, (t + 1) * LB)
        for c in range(CASES):
            low[c, :, cols] = jnp.broadcast_to(-lim[:, cols] - slots_o[t, c : c + 1, :], (8, LB))
            high[c, :, cols] = jnp.broadcast_to(lim[:, cols] - slots_o[t, c : c + 1, :], (8, LB))
    dsum[...] = jnp.zeros_like(dsum)
    qsum[...] = jnp.zeros_like(qsum)
    ids = lax.broadcasted_iota(jnp.int32, (n_tiles, n_tiles), 0)
    place = lax.broadcasted_iota(jnp.int32, (n_tiles, n_tiles), 1)
    listed = (list_ref[...] == ids) & (place < count_ref[...])
    flags = jnp.sum(jnp.where(listed, 1.0, 0.0), axis=1, keepdims=True)
    act[...] = jnp.broadcast_to(flags, (n_tiles, LB))

    def take_falls(m):
        first, many = FALL_PIECES[m]
        for i in range(n_line - 1):
            falls[m][i].wait_recv()
        for b in range(first, first + many):
            total = picked[b]
            for i in range(n_line - 1):
                total = total + recv_l[i, b]
            slots_l[b] = total
            turned[b * LB : (b + 1) * LB, 0:CASES] = total.T

    lanes = lax.broadcasted_iota(jnp.int32, (TILE, LB), 1)

    def tile_step(tile, _):
        k0 = pl.multiple_of(tile * TILE, TILE)
        rows = pl.ds(k0, TILE)
        on = act[pl.ds(tile, 1), :]
        pair = slots_l[tile // 2]
        mine = jnp.where(lax.rem(tile, 2) == 0, pair[:, :TILE], pair[:, TILE:]) * on[:, :TILE]
        qsum[...] += add3(jnp.dot(split3(mine), of[rows, :], preferred_element_type=F32))
        masked = turned[rows, :] * on
        for c in range(CASES):
            fall[c] = jnp.broadcast_to(masked[:, c : c + 1], (TILE, LB))

        def reduce_rows(c, sums):
            return jnp.where(lanes == c, jnp.sum(fall[jnp.maximum(c, 0)], axis=1, keepdims=True), sums)

        def case_step(c):
            ffs = fall[c]
            acc = ffs * square[rows, :]
            for t in range(n_out):
                cols = slice(t * LB, (t + 1) * LB)
                lo = jnp.concatenate([low[c, :, cols]] * n_sub, axis=0)
                hi = jnp.concatenate([high[c, :, cols]] * n_sub, axis=0)
                o = wide_of[rows, cols]
                q = jnp.minimum(jnp.maximum(ffs * o, lo), hi)
                acc = acc - q * o
                size = TILE // 2
                while size >= 8:
                    q = q[:size] + q[size:]
                    size //= 2
                dsum[c, :, cols] += q
            fall[c] = acc

        def group_step(g, sums):
            for e in range(GROUP):
                sums = reduce_rows(g * GROUP - GROUP + e, sums)
            for e in range(GROUP):
                case_step(g * GROUP + e)
            return sums

        sums = lax.fori_loop(0, CASES // GROUP, group_step, jnp.zeros((TILE, LB), F32))
        for e in range(GROUP):
            sums = reduce_rows(CASES - GROUP + e, sums)
        rsum[rows, :] = sums * on
        return 0

    turns = [[message(rev, recv_r, s_rr, m, i, TERM_PIECES[m]) for i in range(n_line - 1)] for m in range(3)]

    def block_step(b, _):
        for m in range(3):

            @pl.when(b == FALL_PIECES[m][0])
            def _():
                take_falls(m)

        lax.fori_loop(b * (LB // TILE), (b + 1) * (LB // TILE), tile_step, 0)
        rev[b] = rsum[pl.ds(pl.multiple_of(b * LB, LB), LB), :].T[:CASES]
        for m in range(3):

            @pl.when(b == sum(TERM_PIECES[m]) - 1)
            def _():
                for copy in turns[m]:
                    copy.start()

        return 0

    lax.fori_loop(0, n_line, block_step, 0)

    idle = TILE * (n_tiles - jnp.sum(act[...], axis=0, keepdims=True))
    for t in range(n_out):
        cols = slice(t * LB, (t + 1) * LB)
        rest = jnp.minimum(jnp.maximum(0.0, low[:, 0, cols]), high[:, 0, cols])
        terms[t] = qsum[:, cols] - (jnp.sum(dsum[:, :, cols], axis=1) - idle * rest)

    def summed(m):
        first, many = TERM_PIECES[m]
        for i in range(n_line - 1):
            turns[m][i].wait_recv()
        blocks = []
        for b in range(first, first + many):
            total = rev[b]
            for i in range(n_line - 1):
                total = total + recv_r[i, b]
            blocks.append(total)
        return blocks

    def placed(three, d, cols):
        table = hot[pl.ds(pl.multiple_of(d * LB, LB), LB), cols]
        return add3(lax.dot_general(three, table, (((1,), (1,)), ((), ())), preferred_element_type=F32))

    early = split3(jnp.concatenate(summed(0) + summed(1), axis=1))
    for t in range(n_out):
        terms[t] += placed(early, t, slice(0, n_k - LB))
    late = split3(summed(2)[0])

    def fill(d):
        terms[d] += placed(late, d, slice(n_k - LB, n_k))

    scattered = send_parts(terms, recv_t, s_rt, "out", fill)
    grad = sum_parts(terms, recv_t, scattered, "out")
    slots_g[me_out] = (grad * (2.0 / NO)).astype(BF16)
    sent += scattered + spread(slots_g, s_gg, "out")
    rounded = jnp.concatenate([slots_g[i] for i in range(n_out)], axis=1)
    partial = jnp.dot(rounded, sf[...], preferred_element_type=F32)
    slots_f[me_line] = partial.astype(BF16)
    sent += spread(slots_f, s_gf, "line")
    result = slots_f[0].astype(F32)
    for i in range(1, n_line):
        result = result + slots_f[i].astype(F32)
    out_ref[...] = result
    for piece in falls + turns:
        finish(piece)
    finish(sent)


def shards(
    n_line, n_out, injections, shift_factors, outage_factors, limits, outage_line, tile_list, tile_count
):
    n_k = n_line * LB
    n_l = n_out * LB
    block = (CASES, LB)
    dma = pltpu.SemaphoreType.DMA
    line_row = outage_line.reshape(1, n_k)
    limit_row = limits.reshape(1, n_l)
    per_line = pltpu.VMEM((n_line,) + block, F32)
    per_out = pltpu.VMEM((n_out,) + block, F32)
    return pl.pallas_call(
        functools.partial(gradient_kernel, n_line, n_out),
        in_specs=[HBM] * 5 + [VMEM] * 2,
        out_specs=VMEM,
        out_shape=jax.ShapeDtypeStruct((CASES, shift_factors.shape[1]), F32),
        scratch_shapes=[
            pltpu.VMEM(injections.shape, BF16),
            pltpu.VMEM(shift_factors.shape, BF16),
            pltpu.VMEM(outage_factors.shape, BF16),
            pltpu.VMEM(limit_row.shape, F32),
            pltpu.VMEM(line_row.shape, jnp.int32),
            per_out,
            per_out,
            per_out,
            pltpu.VMEM((n_l, n_k), BF16),
            per_line,
            pltpu.VMEM((n_line - 1, n_line) + block, F32),
            per_line,
            pltpu.VMEM((n_k, n_l), F32),
            pltpu.VMEM((n_k, LB), F32),
            pltpu.VMEM((CASES, 8, n_l), F32),
            pltpu.VMEM((CASES, 8, n_l), F32),
            pltpu.VMEM((CASES, TILE, LB), F32),
            pltpu.VMEM((CASES, 8, n_l), F32),
            pltpu.VMEM((CASES, n_l), F32),
            pltpu.VMEM((n_k, LB), F32),
            pltpu.VMEM((n_k, LB), F32),
            pltpu.VMEM((n_k // TILE, LB), F32),
            per_line,
            pltpu.VMEM((n_line - 1, n_line) + block, F32),
            per_out,
            per_out,
            pltpu.VMEM((n_out,) + block, BF16),
            pltpu.VMEM((n_line, CASES, shift_factors.shape[1]), BF16),
            dma((5,)),
            dma((2, n_out)),
            dma((2, n_out)),
            dma((2, 3, n_line)),
            dma((2, 3, n_line)),
            dma((2, n_out)),
            dma((2, n_out)),
            dma((2, n_line)),
        ],
        compiler_params=pltpu.CompilerParams(
            collective_id=0, has_side_effects=True, vmem_limit_bytes=63 * 2**20
        ),
        name="gradient",
    )(injections, shift_factors, outage_factors, limit_row, line_row, tile_list, tile_count.reshape(1, 1))


def solution(mesh):
    placed = (
        P(None, "out"),
        P("line", "out"),
        P("out", "line"),
        P("line"),
        P("out"),
        P("out", None),
        P("out"),
    )
    return jax.shard_map(
        functools.partial(shards, mesh.shape["line"], mesh.shape["out"]),
        mesh=mesh,
        in_specs=placed,
        out_specs=P(None, "out"),
        check_vma=False,
    )
```

```python
import functools

import jax
import jax.numpy as jnp
from jax import lax
from jax.experimental import pallas as pl
from jax.experimental.pallas import tpu as pltpu
from jax.sharding import PartitionSpec as P

CASES = 32
NO = 16384
TILE = 64
GROUP = 4
LB = 128
F32 = jnp.float32
BF16 = jnp.bfloat16
MESH = pl.DeviceIdType.MESH
VMEM = pl.BlockSpec(memory_space=pltpu.VMEM)
HBM = pl.BlockSpec(memory_space=pltpu.HBM)


LINE_STEPS = [(1, 2), (1, 1), (1, 3), (0, 2), (1, 0), (0, 1), (0, 3)]
OUT_STEPS = [(x, y, c) for x, y in [(1, 2), (1, 1), (1, 3), (0, 2), (1, 0), (0, 1), (0, 3)] for c in (1, 0)]
OUT_STEPS += [(0, 0, 1)]
FALL_PIECES = [(0, 1), (1, 1), (2, 6)]
TERM_PIECES = [(0, 4), (4, 3), (7, 1)]
STEPS = {"line": LINE_STEPS, "out": OUT_STEPS}


def partner(axis, i):
    me = lax.axis_index(axis)
    if axis == "line":
        dx, dz = LINE_STEPS[i]
        return lax.rem(me // 4 + dx, 2) * 4 + lax.rem(lax.rem(me, 4) + dz, 4)
    dx, dy, dc = OUT_STEPS[i]
    x, y, c = me // 8, lax.rem(me // 2, 4), lax.rem(me, 2)
    return lax.rem(x + dx, 2) * 8 + lax.rem(y + dy, 4) * 2 + lax.rem(c + dc, 2)


def peer(axis, i):
    if axis == "out":
        return (lax.axis_index("line"), partner(axis, i))
    return (partner(axis, i), lax.axis_index("out"))


def greet():
    barrier = pltpu.get_barrier_semaphore()
    for axis in ("out", "line"):
        for i in range(len(STEPS[axis])):
            pl.semaphore_signal(barrier, inc=1, device_id=peer(axis, i), device_id_type=MESH)
    return barrier


def send(src, dst, sems, i, axis):
    copy = pltpu.make_async_remote_copy(
        src_ref=src,
        dst_ref=dst,
        send_sem=sems.at[0, i],
        recv_sem=sems.at[1, i],
        device_id=peer(axis, i),
        device_id_type=MESH,
    )
    copy.start()
    return copy


def split3(x):
    hi = x.astype(BF16)
    rest = x - hi.astype(F32)
    mid = rest.astype(BF16)
    low = (rest - mid.astype(F32)).astype(BF16)
    return jnp.concatenate([hi, mid, low], axis=0)


def send_parts(parts, recv, sems, axis):
    return [
        send(parts.at[partner(axis, i)], recv.at[i], sems, i, axis) for i in range(len(STEPS[axis]))
    ]


def sum_parts(parts, recv, copies, axis):
    total = parts[lax.axis_index(axis)]
    for i in reversed(range(len(copies))):
        copies[i].wait_recv()
        total = total + recv[i]
    return total


def finish(copies):
    for copy in copies:
        copy.wait_send()


def spread(slots, sems, axis, meanwhile=None):
    me = lax.axis_index(axis)
    copies = [send(slots.at[me], slots.at[me], sems, i, axis) for i in range(len(STEPS[axis]))]
    if meanwhile is not None:
        meanwhile()
    for copy in copies:
        copy.wait_recv()
    return copies


def hot_table(hot, line_ref, n_out, n_k):
    local = line_ref[...] - lax.axis_index("line") * (n_out * LB)

    def hot_rows(r, _):
        base = pl.multiple_of(r * LB, LB)
        ids = lax.broadcasted_iota(jnp.int32, (LB, n_k), 0) + base
        hot[pl.ds(base, LB), :] = (ids == local).astype(F32).astype(BF16)
        return 0

    lax.fori_loop(0, n_out, hot_rows, 0)


def message(src, dst, sems, m, i, piece):
    return pltpu.make_async_remote_copy(
        src_ref=src.at[pl.ds(*piece)],
        dst_ref=dst.at[i, pl.ds(*piece)],
        send_sem=sems.at[0, m, i],
        recv_sem=sems.at[1, m, i],
        device_id=peer("line", i),
        device_id_type=MESH,
    )


def add3(x):
    return x[:CASES] + x[CASES : 2 * CASES] + x[2 * CASES :]


def gradient_kernel(
    n_line, n_out, inj_hbm, sf_hbm, of_hbm, lim_hbm, line_hbm, list_ref, count_ref, out_ref,
    inj, sf, of, lim, line, parts, recv_o, slots_o, hot, picked, recv_l, slots_l,
    wide_of, square, low, high, fall, dsum, qsum, turned, act,
    rev, recv_r, terms, recv_t, slots_g, slots_f,
    s_in, s_ro, s_go, s_rl, s_rr, s_rt, s_gg, s_gf,
):
    n_k = n_line * LB
    n_tiles = n_k // TILE
    me_line = lax.axis_index("line")
    me_out = lax.axis_index("out")
    loads = [
        pltpu.make_async_copy(src, dst, s_in.at[i])
        for i, (src, dst) in enumerate(
            [(inj_hbm, inj), (sf_hbm, sf), (line_hbm, line), (lim_hbm, lim), (of_hbm, of)]
        )
    ]
    for load in loads:
        load.start()
    barrier = greet()

    def widen(first, last):
        def one(tile, _):
            rows = pl.ds(pl.multiple_of(tile * TILE, TILE), TILE)
            total = jnp.zeros((TILE, LB), F32)
            for t in range(n_out):
                w = of[rows, t * LB : (t + 1) * LB].astype(F32)
                wide_of[rows, t * LB : (t + 1) * LB] = w
                total = total + w * w
            square[rows, :] = total
            return 0

        lax.fori_loop(first, last, one, 0)

    loads[0].wait()
    loads[1].wait()
    partial = lax.dot_general(inj[...], sf[...], (((1,), (1,)), ((), ())), preferred_element_type=F32)
    for d in range(n_out):
        parts[d] = partial[:, d * LB : (d + 1) * LB]
    pl.semaphore_wait(barrier, n_out + n_line - 2)
    sent = send_parts(parts, recv_o, s_ro, "out")
    for load in loads[2:]:
        load.wait()
    hot_table(hot, line, n_out, n_k)
    widen(0, n_tiles // 2)
    slots_o[me_out] = sum_parts(parts, recv_o, sent, "out")
    sent += spread(slots_o, s_go, "out", lambda: widen(n_tiles // 2, n_tiles))
    flow = split3(jnp.concatenate([slots_o[i] for i in range(n_out)], axis=1))
    falls = [[message(picked, recv_l, s_rl, m, i, FALL_PIECES[m]) for i in range(n_line - 1)] for m in range(3)]
    for m in range(3):
        first, many = FALL_PIECES[m]
        got = add3(
            jnp.dot(flow, hot[:, first * LB : (first + many) * LB], preferred_element_type=F32)
        )
        for i in range(many):
            picked[first + i] = got[:, i * LB : (i + 1) * LB]
        for copy in falls[m]:
            copy.start()
    for t in range(n_out):
        cols = slice(t * LB, (t + 1) * LB)
        for c in range(CASES):
            low[c, :, cols] = jnp.broadcast_to(-lim[:, cols] - slots_o[t, c : c + 1, :], (8, LB))
            high[c, :, cols] = jnp.broadcast_to(lim[:, cols] - slots_o[t, c : c + 1, :], (8, LB))
    dsum[...] = jnp.zeros_like(dsum)
    qsum[...] = jnp.zeros_like(qsum)
    ids = lax.broadcasted_iota(jnp.int32, (n_tiles, n_tiles), 0)
    place = lax.broadcasted_iota(jnp.int32, (n_tiles, n_tiles), 1)
    listed = (list_ref[...] == ids) & (place < count_ref[...])
    flags = jnp.sum(jnp.where(listed, 1.0, 0.0), axis=1, keepdims=True)
    act[...] = jnp.broadcast_to(flags, (n_tiles, LB))

    def take_falls(m):
        first, many = FALL_PIECES[m]
        for i in range(n_line - 1):
            falls[m][i].wait_recv()
        for b in range(first, first + many):
            total = picked[b]
            for i in range(n_line - 1):
                total = total + recv_l[i, b]
            slots_l[b] = total
            turned[b * LB : (b + 1) * LB, 0:CASES] = total.T

    lanes = lax.broadcasted_iota(jnp.int32, (LB, LB), 1)
    n_sub = LB // 8

    def terms_of_block(b):
        k0 = pl.multiple_of(b * LB, LB)
        rows = pl.ds(k0, LB)
        on_a = act[pl.ds(2 * b, 1), :]
        on_b = act[pl.ds(2 * b + 1, 1), :]
        on = jnp.concatenate([jnp.broadcast_to(on_a, (TILE, LB)), jnp.broadcast_to(on_b, (TILE, LB))], axis=0)
        mine = slots_l[b] * jnp.where(lanes[0:1] < TILE, on_a, on_b)
        qsum[...] += add3(jnp.dot(split3(mine), of[rows, :], preferred_element_type=F32))
        masked = turned[rows, :] * on
        for c in range(CASES):
            fall[c] = jnp.broadcast_to(masked[:, c : c + 1], (LB, LB))

        def reduce_rows(c, sums):
            return jnp.where(lanes == c, jnp.sum(fall[jnp.maximum(c, 0)], axis=1, keepdims=True), sums)

        def case_step(c):
            ffs = [fall[c, 8 * i : 8 * i + 8, :] for i in range(n_sub)]
            acc = [ffs[i] * square[pl.ds(k0 + 8 * i, 8), :] for i in range(n_sub)]
            for t in range(n_out):
                cols = slice(t * LB, (t + 1) * LB)
                lo = low[c, :, cols]
                hi = high[c, :, cols]
                total = None
                for i in range(0, n_sub, 2):
                    pair = []
                    for j in (i, i + 1):
                        o = wide_of[pl.ds(k0 + 8 * j, 8), cols]
                        q = jnp.minimum(jnp.maximum(ffs[j] * o, lo), hi)
                        acc[j] = acc[j] - q * o
                        pair.append(q)
                    both = pair[0] + pair[1]
                    total = both if total is None else total + both
                dsum[c, :, cols] += total
            for i in range(n_sub):
                fall[c, 8 * i : 8 * i + 8, :] = acc[i]

        def group_step(g, sums):
            for e in range(GROUP):
                sums = reduce_rows(g * GROUP - GROUP + e, sums)
            for e in range(GROUP):
                case_step(g * GROUP + e)
            return sums

        sums = lax.fori_loop(0, CASES // GROUP, group_step, jnp.zeros((LB, LB), F32))
        for e in range(GROUP):
            sums = reduce_rows(CASES - GROUP + e, sums)
        rev[b] = (sums * on).T[:CASES]

    turns = [[message(rev, recv_r, s_rr, m, i, TERM_PIECES[m]) for i in range(n_line - 1)] for m in range(3)]

    def block_step(b, _):
        for m in range(3):

            @pl.when(b == FALL_PIECES[m][0])
            def _():
                take_falls(m)

        terms_of_block(b)
        for m in range(3):

            @pl.when(b == sum(TERM_PIECES[m]) - 1)
            def _():
                for copy in turns[m]:
                    copy.start()

        return 0

    lax.fori_loop(0, n_line, block_step, 0)

    idle = TILE * (n_tiles - jnp.sum(act[...], axis=0, keepdims=True))
    for t in range(n_out):
        cols = slice(t * LB, (t + 1) * LB)
        rest = jnp.minimum(jnp.maximum(0.0, low[:, 0, cols]), high[:, 0, cols])
        terms[t] = qsum[:, cols] - (jnp.sum(dsum[:, :, cols], axis=1) - idle * rest)

    def summed(m):
        first, many = TERM_PIECES[m]
        for i in range(n_line - 1):
            turns[m][i].wait_recv()
        blocks = []
        for b in range(first, first + many):
            total = rev[b]
            for i in range(n_line - 1):
                total = total + recv_r[i, b]
            blocks.append(total)
        return blocks

    def place(three, cols):
        got = add3(
            lax.dot_general(three, hot[:, cols], (((1,), (1,)), ((), ())), preferred_element_type=F32)
        )
        for t in range(n_out):
            terms[t] += got[:, t * LB : (t + 1) * LB]

    place(split3(jnp.concatenate(summed(0) + summed(1), axis=1)), slice(0, n_k - LB))
    place(split3(summed(2)[0]), slice(n_k - LB, n_k))
    scattered = send_parts(terms, recv_t, s_rt, "out")
    grad = sum_parts(terms, recv_t, scattered, "out")
    slots_g[me_out] = (grad * (2.0 / NO)).astype(BF16)
    sent += scattered + spread(slots_g, s_gg, "out")
    rounded = jnp.concatenate([slots_g[i] for i in range(n_out)], axis=1)
    partial = jnp.dot(rounded, sf[...], preferred_element_type=F32)
    slots_f[me_line] = partial.astype(BF16)
    sent += spread(slots_f, s_gf, "line")
    result = slots_f[0].astype(F32)
    for i in range(1, n_line):
        result = result + slots_f[i].astype(F32)
    out_ref[...] = result
    for piece in falls + turns:
        finish(piece)
    finish(sent)


def shards(
    n_line, n_out, injections, shift_factors, outage_factors, limits, outage_line, tile_list, tile_count
):
    n_k = n_line * LB
    n_l = n_out * LB
    block = (CASES, LB)
    dma = pltpu.SemaphoreType.DMA
    line_row = outage_line.reshape(1, n_k)
    limit_row = limits.reshape(1, n_l)
    per_line = pltpu.VMEM((n_line,) + block, F32)
    per_out = pltpu.VMEM((n_out,) + block, F32)
    return pl.pallas_call(
        functools.partial(gradient_kernel, n_line, n_out),
        in_specs=[HBM] * 5 + [VMEM] * 2,
        out_specs=VMEM,
        out_shape=jax.ShapeDtypeStruct((CASES, shift_factors.shape[1]), F32),
        scratch_shapes=[
            pltpu.VMEM(injections.shape, BF16),
            pltpu.VMEM(shift_factors.shape, BF16),
            pltpu.VMEM(outage_factors.shape, BF16),
            pltpu.VMEM(limit_row.shape, F32),
            pltpu.VMEM(line_row.shape, jnp.int32),
            per_out,
            per_out,
            per_out,
            pltpu.VMEM((n_l, n_k), BF16),
            per_line,
            pltpu.VMEM((n_line - 1, n_line) + block, F32),
            per_line,
            pltpu.VMEM((n_k, n_l), F32),
            pltpu.VMEM((n_k, LB), F32),
            pltpu.VMEM((CASES, 8, n_l), F32),
            pltpu.VMEM((CASES, 8, n_l), F32),
            pltpu.VMEM((CASES, LB, LB), F32),
            pltpu.VMEM((CASES, 8, n_l), F32),
            pltpu.VMEM((CASES, n_l), F32),
            pltpu.VMEM((n_k, LB), F32),
            pltpu.VMEM((n_k // TILE, LB), F32),
            per_line,
            pltpu.VMEM((n_line - 1, n_line) + block, F32),
            per_out,
            per_out,
            pltpu.VMEM((n_out,) + block, BF16),
            pltpu.VMEM((n_line, CASES, shift_factors.shape[1]), BF16),
            dma((5,)),
            dma((2, n_out)),
            dma((2, n_out)),
            dma((2, 3, n_line)),
            dma((2, 3, n_line)),
            dma((2, n_out)),
            dma((2, n_out)),
            dma((2, n_line)),
        ],
        compiler_params=pltpu.CompilerParams(
            collective_id=0, has_side_effects=True, vmem_limit_bytes=63 * 2**20
        ),
        name="gradient",
    )(injections, shift_factors, outage_factors, limit_row, line_row, tile_list, tile_count.reshape(1, 1))


def solution(mesh):
    placed = (
        P(None, "out"),
        P("line", "out"),
        P("out", "line"),
        P("line"),
        P("out"),
        P("out", None),
        P("out"),
    )
    return jax.shard_map(
        functools.partial(shards, mesh.shape["line"], mesh.shape["out"]),
        mesh=mesh,
        in_specs=placed,
        out_specs=P(None, "out"),
        check_vma=False,
    )
```

```python
import functools

import jax
import jax.numpy as jnp
from jax import lax
from jax.experimental import pallas as pl
from jax.experimental.pallas import tpu as pltpu
from jax.sharding import PartitionSpec as P

CASES = 32
NO = 16384
TILE = 64
GROUP = 4
LB = 128
F32 = jnp.float32
BF16 = jnp.bfloat16
MESH = pl.DeviceIdType.MESH
VMEM = pl.BlockSpec(memory_space=pltpu.VMEM)
HBM = pl.BlockSpec(memory_space=pltpu.HBM)


LINE_STEPS = [(1, 2), (1, 1), (1, 3), (0, 2), (1, 0), (0, 1), (0, 3)]
OUT_STEPS = [(x, y, c) for x, y in [(1, 2), (1, 1), (1, 3), (0, 2), (1, 0), (0, 1), (0, 3)] for c in (1, 0)]
OUT_STEPS += [(0, 0, 1)]
FALL_PIECES = [(0, 1), (1, 1), (2, 6)]
TERM_PIECES = [(0, 4), (4, 3), (7, 1)]
STEPS = {"line": LINE_STEPS, "out": OUT_STEPS}


def partner(axis, i):
    me = lax.axis_index(axis)
    if axis == "line":
        dx, dz = LINE_STEPS[i]
        return lax.rem(me // 4 + dx, 2) * 4 + lax.rem(lax.rem(me, 4) + dz, 4)
    dx, dy, dc = OUT_STEPS[i]
    x, y, c = me // 8, lax.rem(me // 2, 4), lax.rem(me, 2)
    return lax.rem(x + dx, 2) * 8 + lax.rem(y + dy, 4) * 2 + lax.rem(c + dc, 2)


def peer(axis, i):
    if axis == "out":
        return (lax.axis_index("line"), partner(axis, i))
    return (partner(axis, i), lax.axis_index("out"))


def greet():
    barrier = pltpu.get_barrier_semaphore()
    for axis in ("out", "line"):
        for i in range(len(STEPS[axis])):
            pl.semaphore_signal(barrier, inc=1, device_id=peer(axis, i), device_id_type=MESH)
    return barrier


def send(src, dst, sems, i, axis):
    copy = pltpu.make_async_remote_copy(
        src_ref=src,
        dst_ref=dst,
        send_sem=sems.at[0, i],
        recv_sem=sems.at[1, i],
        device_id=peer(axis, i),
        device_id_type=MESH,
    )
    copy.start()
    return copy


def split3(x):
    hi = x.astype(BF16)
    rest = x - hi.astype(F32)
    mid = rest.astype(BF16)
    low = (rest - mid.astype(F32)).astype(BF16)
    return jnp.concatenate([hi, mid, low], axis=0)


def send_parts(parts, recv, sems, axis):
    return [
        send(parts.at[partner(axis, i)], recv.at[i], sems, i, axis) for i in range(len(STEPS[axis]))
    ]


def sum_parts(parts, recv, copies, axis):
    total = parts[lax.axis_index(axis)]
    for i in reversed(range(len(copies))):
        copies[i].wait_recv()
        total = total + recv[i]
    return total


def finish(copies):
    for copy in copies:
        copy.wait_send()


def spread(slots, sems, axis, meanwhile=None):
    me = lax.axis_index(axis)
    copies = [send(slots.at[me], slots.at[me], sems, i, axis) for i in range(len(STEPS[axis]))]
    if meanwhile is not None:
        meanwhile()
    for copy in copies:
        copy.wait_recv()
    return copies


def hot_table(hot, line_ref, n_out, n_k):
    local = line_ref[...] - lax.axis_index("line") * (n_out * LB)

    def hot_rows(r, _):
        base = pl.multiple_of(r * LB, LB)
        ids = lax.broadcasted_iota(jnp.int32, (LB, n_k), 0) + base
        hot[pl.ds(base, LB), :] = (ids == local).astype(F32).astype(BF16)
        return 0

    lax.fori_loop(0, n_out, hot_rows, 0)


def message(src, dst, sems, m, i, piece):
    return pltpu.make_async_remote_copy(
        src_ref=src.at[pl.ds(*piece)],
        dst_ref=dst.at[i, pl.ds(*piece)],
        send_sem=sems.at[0, m, i],
        recv_sem=sems.at[1, m, i],
        device_id=peer("line", i),
        device_id_type=MESH,
    )


def add3(x):
    return x[:CASES] + x[CASES : 2 * CASES] + x[2 * CASES :]


def gradient_kernel(
    n_line, n_out, inj_hbm, sf_hbm, of_hbm, lim_hbm, line_hbm, list_ref, count_ref, out_ref,
    inj, sf, of, lim, line, parts, recv_o, slots_o, hot, picked, recv_l, slots_l,
    wide_of, square, low, high, fall, dsum, turned, act,
    rev, recv_r, terms, recv_t, slots_g, slots_f,
    s_in, s_ro, s_go, s_rl, s_rr, s_rt, s_gg, s_gf,
):
    n_k = n_line * LB
    n_tiles = n_k // TILE
    me_line = lax.axis_index("line")
    me_out = lax.axis_index("out")
    loads = [
        pltpu.make_async_copy(src, dst, s_in.at[i])
        for i, (src, dst) in enumerate(
            [(inj_hbm, inj), (sf_hbm, sf), (line_hbm, line), (lim_hbm, lim), (of_hbm, of)]
        )
    ]
    barrier = greet()
    for load in loads[:4]:
        load.start()

    def widen(first, last):
        def one(tile, _):
            rows = pl.ds(pl.multiple_of(tile * TILE, TILE), TILE)
            total = jnp.zeros((TILE, LB), F32)
            for t in range(n_out):
                w = of[rows, t * LB : (t + 1) * LB].astype(F32)
                wide_of[rows, t * LB : (t + 1) * LB] = w
                total = total + w * w
            square[rows, :] = total
            return 0

        lax.fori_loop(first, last, one, 0)

    loads[0].wait()
    loads[1].wait()
    loads[4].start()
    partial = lax.dot_general(inj[...], sf[...], (((1,), (1,)), ((), ())), preferred_element_type=F32)
    for d in range(n_out):
        parts[d] = partial[:, d * LB : (d + 1) * LB]
    pl.semaphore_wait(barrier, n_out + n_line - 2)
    sent = send_parts(parts, recv_o, s_ro, "out")
    for load in loads[2:]:
        load.wait()
    hot_table(hot, line, n_out, n_k)
    widen(0, n_tiles // 2 - 1)
    slots_o[me_out] = sum_parts(parts, recv_o, sent, "out")
    sent += spread(slots_o, s_go, "out", lambda: widen(n_tiles // 2 - 1, n_tiles))
    flow = split3(jnp.concatenate([slots_o[i] for i in range(n_out)], axis=1))
    falls = [[message(picked, recv_l, s_rl, m, i, FALL_PIECES[m]) for i in range(n_line - 1)] for m in range(3)]
    for m in range(3):
        first, many = FALL_PIECES[m]
        got = add3(
            jnp.dot(flow, hot[:, first * LB : (first + many) * LB], preferred_element_type=F32)
        )
        for i in range(many):
            picked[first + i] = got[:, i * LB : (i + 1) * LB]
        for copy in falls[m]:
            copy.start()
    for t in range(n_out):
        cols = slice(t * LB, (t + 1) * LB)
        for c in range(CASES):
            low[c, :, cols] = jnp.broadcast_to(-lim[:, cols] - slots_o[t, c : c + 1, :], (8, LB))
            high[c, :, cols] = jnp.broadcast_to(lim[:, cols] - slots_o[t, c : c + 1, :], (8, LB))
    dsum[...] = jnp.zeros_like(dsum)
    ids = lax.broadcasted_iota(jnp.int32, (n_tiles, n_tiles), 0)
    place = lax.broadcasted_iota(jnp.int32, (n_tiles, n_tiles), 1)
    listed = (list_ref[...] == ids) & (place < count_ref[...])
    flags = jnp.sum(jnp.where(listed, 1.0, 0.0), axis=1, keepdims=True)
    act[...] = jnp.broadcast_to(flags, (n_tiles, LB))

    def take_falls(m):
        first, many = FALL_PIECES[m]
        for i in range(n_line - 1):
            falls[m][i].wait_recv()
        for b in range(first, first + many):
            total = picked[b]
            for i in range(n_line - 1):
                total = total + recv_l[i, b]
            slots_l[b] = total
            turned[b * LB : (b + 1) * LB, 0:CASES] = total.T

    lanes = lax.broadcasted_iota(jnp.int32, (LB, LB), 1)
    n_sub = LB // 8

    def terms_of_block(b):
        k0 = pl.multiple_of(b * LB, LB)
        rows = pl.ds(k0, LB)
        on_a = act[pl.ds(2 * b, 1), :]
        on_b = act[pl.ds(2 * b + 1, 1), :]
        on = jnp.concatenate([jnp.broadcast_to(on_a, (TILE, LB)), jnp.broadcast_to(on_b, (TILE, LB))], axis=0)
        masked = turned[rows, :] * on
        for c in range(CASES):
            fall[c] = jnp.broadcast_to(masked[:, c : c + 1], (LB, LB))

        def reduce_rows(c, sums):
            return jnp.where(lanes == c, jnp.sum(fall[jnp.maximum(c, 0)], axis=1, keepdims=True), sums)

        def case_step(c):
            ffs = [fall[c, 8 * i : 8 * i + 8, :] for i in range(n_sub)]
            acc = [ffs[i] * square[pl.ds(k0 + 8 * i, 8), :] for i in range(n_sub)]
            for t in range(n_out):
                cols = slice(t * LB, (t + 1) * LB)
                lo = low[c, :, cols]
                hi = high[c, :, cols]
                total = None
                for i in range(0, n_sub, 2):
                    pair = []
                    for j in (i, i + 1):
                        o = wide_of[pl.ds(k0 + 8 * j, 8), cols]
                        q = jnp.minimum(jnp.maximum(ffs[j] * o, lo), hi)
                        acc[j] = acc[j] - q * o
                        pair.append(q)
                    both = pair[0] + pair[1]
                    total = both if total is None else total + both
                dsum[c, :, cols] += total
            for i in range(n_sub):
                fall[c, 8 * i : 8 * i + 8, :] = acc[i]

        def group_step(g, sums):
            for e in range(GROUP):
                sums = reduce_rows(g * GROUP - GROUP + e, sums)
            for e in range(GROUP):
                case_step(g * GROUP + e)
            return sums

        sums = lax.fori_loop(0, CASES // GROUP, group_step, jnp.zeros((LB, LB), F32))
        for e in range(GROUP):
            sums = reduce_rows(CASES - GROUP + e, sums)
        rev[b] = (sums * on).T[:CASES]

    turns = [[message(rev, recv_r, s_rr, m, i, TERM_PIECES[m]) for i in range(n_line - 1)] for m in range(3)]

    def block_step(b, _):
        for m in range(3):

            @pl.when(b == FALL_PIECES[m][0])
            def _():
                take_falls(m)

        terms_of_block(b)
        for m in range(3):

            @pl.when(b == sum(TERM_PIECES[m]) - 1)
            def _():
                for copy in turns[m]:
                    copy.start()

        return 0

    lax.fori_loop(0, n_line, block_step, 0)

    falling = []
    for b in range(n_line):
        on = jnp.where(lanes[0:1] < TILE, act[2 * b : 2 * b + 1, :], act[2 * b + 1 : 2 * b + 2, :])
        falling.append(slots_l[b] * on)
    qsum = add3(jnp.dot(split3(jnp.concatenate(falling, axis=1)), of[...], preferred_element_type=F32))
    idle = TILE * (n_tiles - jnp.sum(act[...], axis=0, keepdims=True))
    for t in range(n_out):
        cols = slice(t * LB, (t + 1) * LB)
        rest = jnp.minimum(jnp.maximum(0.0, low[:, 0, cols]), high[:, 0, cols])
        terms[t] = qsum[:, cols] - (jnp.sum(dsum[:, :, cols], axis=1) - idle * rest)

    def summed(m):
        first, many = TERM_PIECES[m]
        for i in range(n_line - 1):
            turns[m][i].wait_recv()
        blocks = []
        for b in range(first, first + many):
            total = rev[b]
            for i in range(n_line - 1):
                total = total + recv_r[i, b]
            blocks.append(total)
        return blocks

    def place(three, cols):
        got = add3(
            lax.dot_general(three, hot[:, cols], (((1,), (1,)), ((), ())), preferred_element_type=F32)
        )
        for t in range(n_out):
            terms[t] += got[:, t * LB : (t + 1) * LB]

    place(split3(jnp.concatenate(summed(0) + summed(1), axis=1)), slice(0, n_k - LB))
    place(split3(summed(2)[0]), slice(n_k - LB, n_k))
    scattered = send_parts(terms, recv_t, s_rt, "out")
    grad = sum_parts(terms, recv_t, scattered, "out")
    slots_g[me_out] = (grad * (2.0 / NO)).astype(BF16)
    sent += scattered + spread(slots_g, s_gg, "out")
    rounded = jnp.concatenate([slots_g[i] for i in range(n_out)], axis=1)
    partial = jnp.dot(rounded, sf[...], preferred_element_type=F32)
    slots_f[me_line] = partial.astype(BF16)
    sent += spread(slots_f, s_gf, "line")
    result = slots_f[0].astype(F32)
    for i in range(1, n_line):
        result = result + slots_f[i].astype(F32)
    out_ref[...] = result
    for piece in falls + turns:
        finish(piece)
    finish(sent)


def shards(
    n_line, n_out, injections, shift_factors, outage_factors, limits, outage_line, tile_list, tile_count
):
    n_k = n_line * LB
    n_l = n_out * LB
    block = (CASES, LB)
    dma = pltpu.SemaphoreType.DMA
    line_row = outage_line.reshape(1, n_k)
    limit_row = limits.reshape(1, n_l)
    per_line = pltpu.VMEM((n_line,) + block, F32)
    per_out = pltpu.VMEM((n_out,) + block, F32)
    return pl.pallas_call(
        functools.partial(gradient_kernel, n_line, n_out),
        in_specs=[HBM] * 5 + [VMEM] * 2,
        out_specs=VMEM,
        out_shape=jax.ShapeDtypeStruct((CASES, shift_factors.shape[1]), F32),
        scratch_shapes=[
            pltpu.VMEM(injections.shape, BF16),
            pltpu.VMEM(shift_factors.shape, BF16),
            pltpu.VMEM(outage_factors.shape, BF16),
            pltpu.VMEM(limit_row.shape, F32),
            pltpu.VMEM(line_row.shape, jnp.int32),
            per_out,
            per_out,
            per_out,
            pltpu.VMEM((n_l, n_k), BF16),
            per_line,
            pltpu.VMEM((n_line - 1, n_line) + block, F32),
            per_line,
            pltpu.VMEM((n_k, n_l), F32),
            pltpu.VMEM((n_k, LB), F32),
            pltpu.VMEM((CASES, 8, n_l), F32),
            pltpu.VMEM((CASES, 8, n_l), F32),
            pltpu.VMEM((CASES, LB, LB), F32),
            pltpu.VMEM((CASES, 8, n_l), F32),
            pltpu.VMEM((n_k, LB), F32),
            pltpu.VMEM((n_k // TILE, LB), F32),
            per_line,
            pltpu.VMEM((n_line - 1, n_line) + block, F32),
            per_out,
            per_out,
            pltpu.VMEM((n_out,) + block, BF16),
            pltpu.VMEM((n_line, CASES, shift_factors.shape[1]), BF16),
            dma((5,)),
            dma((2, n_out)),
            dma((2, n_out)),
            dma((2, 3, n_line)),
            dma((2, 3, n_line)),
            dma((2, n_out)),
            dma((2, n_out)),
            dma((2, n_line)),
        ],
        compiler_params=pltpu.CompilerParams(
            collective_id=0, has_side_effects=True, vmem_limit_bytes=63 * 2**20
        ),
        name="gradient",
    )(injections, shift_factors, outage_factors, limit_row, line_row, tile_list, tile_count.reshape(1, 1))


def solution(mesh):
    placed = (
        P(None, "out"),
        P("line", "out"),
        P("out", "line"),
        P("line"),
        P("out"),
        P("out", None),
        P("out"),
    )
    return jax.shard_map(
        functools.partial(shards, mesh.shape["line"], mesh.shape["out"]),
        mesh=mesh,
        in_specs=placed,
        out_specs=P(None, "out"),
        check_vma=False,
    )
```

```python
import functools

import jax
import jax.numpy as jnp
from jax import lax
from jax.experimental import pallas as pl
from jax.experimental.pallas import tpu as pltpu
from jax.sharding import PartitionSpec as P

CASES = 32
NO = 16384
TILE = 64
GROUP = 4
LB = 128
F32 = jnp.float32
BF16 = jnp.bfloat16
MESH = pl.DeviceIdType.MESH
VMEM = pl.BlockSpec(memory_space=pltpu.VMEM)
HBM = pl.BlockSpec(memory_space=pltpu.HBM)


LINE_STEPS = [(1, 2), (1, 1), (1, 3), (0, 2), (1, 0), (0, 1), (0, 3)]
OUT_STEPS = [(x, y, c) for x, y in [(1, 2), (1, 1), (1, 3), (0, 2), (1, 0), (0, 1), (0, 3)] for c in (1, 0)]
OUT_STEPS += [(0, 0, 1)]
FALL_PIECES = [(0, 1), (1, 1), (2, 6)]
TERM_PIECES = [(0, 4), (4, 3), (7, 1)]
STEPS = {"line": LINE_STEPS, "out": OUT_STEPS}


def partner(axis, i):
    me = lax.axis_index(axis)
    if axis == "line":
        dx, dz = LINE_STEPS[i]
        return lax.rem(me // 4 + dx, 2) * 4 + lax.rem(lax.rem(me, 4) + dz, 4)
    dx, dy, dc = OUT_STEPS[i]
    x, y, c = me // 8, lax.rem(me // 2, 4), lax.rem(me, 2)
    return lax.rem(x + dx, 2) * 8 + lax.rem(y + dy, 4) * 2 + lax.rem(c + dc, 2)


def peer(axis, i):
    if axis == "out":
        return (lax.axis_index("line"), partner(axis, i))
    return (partner(axis, i), lax.axis_index("out"))


def greet():
    barrier = pltpu.get_barrier_semaphore()
    for axis in ("out", "line"):
        for i in range(len(STEPS[axis])):
            pl.semaphore_signal(barrier, inc=1, device_id=peer(axis, i), device_id_type=MESH)
    return barrier


def send(src, dst, sems, i, axis):
    copy = pltpu.make_async_remote_copy(
        src_ref=src,
        dst_ref=dst,
        send_sem=sems.at[0, i],
        recv_sem=sems.at[1, i],
        device_id=peer(axis, i),
        device_id_type=MESH,
    )
    copy.start()
    return copy


def split3(x):
    hi = x.astype(BF16)
    rest = x - hi.astype(F32)
    mid = rest.astype(BF16)
    low = (rest - mid.astype(F32)).astype(BF16)
    return jnp.concatenate([hi, mid, low], axis=0)


def send_parts(parts, recv, sems, axis):
    return [
        send(parts.at[partner(axis, i)], recv.at[i], sems, i, axis) for i in range(len(STEPS[axis]))
    ]


def sum_parts(parts, recv, copies, axis):
    total = parts[lax.axis_index(axis)]
    for i in reversed(range(len(copies))):
        copies[i].wait_recv()
        total = total + recv[i]
    return total


def finish(copies):
    for copy in copies:
        copy.wait_send()


def spread(slots, sems, axis, meanwhile=None):
    me = lax.axis_index(axis)
    copies = [send(slots.at[me], slots.at[me], sems, i, axis) for i in range(len(STEPS[axis]))]
    if meanwhile is not None:
        meanwhile()
    for copy in copies:
        copy.wait_recv()
    return copies


def hot_table(hot, line_ref, n_out, n_k):
    local = line_ref[...] - lax.axis_index("line") * (n_out * LB)

    def hot_rows(r, _):
        base = pl.multiple_of(r * LB, LB)
        ids = lax.broadcasted_iota(jnp.int32, (LB, n_k), 0) + base
        hot[pl.ds(base, LB), :] = (ids == local).astype(F32).astype(BF16)
        return 0

    lax.fori_loop(0, n_out, hot_rows, 0)


def message(src, dst, sems, m, i, piece):
    return pltpu.make_async_remote_copy(
        src_ref=src.at[pl.ds(*piece)],
        dst_ref=dst.at[i, pl.ds(*piece)],
        send_sem=sems.at[0, m, i],
        recv_sem=sems.at[1, m, i],
        device_id=peer("line", i),
        device_id_type=MESH,
    )


def add3(x):
    return x[:CASES] + x[CASES : 2 * CASES] + x[2 * CASES :]


def gradient_kernel(
    n_line, n_out, inj_hbm, sf_hbm, of_hbm, lim_hbm, line_hbm, list_ref, count_ref, out_ref,
    inj, sf, of, lim, line, parts, recv_o, slots_o, hot, picked, recv_l, slots_l,
    wide_of, square, low, high, fall, dsum, turned, act,
    rev, recv_r, terms, recv_t, slots_g, slots_f,
    s_in, s_ro, s_go, s_rl, s_rr, s_rt, s_gg, s_gf,
):
    n_k = n_line * LB
    n_tiles = n_k // TILE
    me_line = lax.axis_index("line")
    me_out = lax.axis_index("out")
    n_half = n_out * LB // 2
    loads = [
        pltpu.make_async_copy(src, dst, s_in.at[i])
        for i, (src, dst) in enumerate(
            [
                (inj_hbm, inj),
                (sf_hbm.at[pl.ds(0, n_half)], sf.at[pl.ds(0, n_half)]),
                (sf_hbm.at[pl.ds(n_half, n_half)], sf.at[pl.ds(n_half, n_half)]),
                (line_hbm, line),
                (lim_hbm, lim),
                (of_hbm, of),
            ]
        )
    ]
    barrier = greet()
    for load in loads[:5]:
        load.start()

    def widen(first, last):
        def one(tile, _):
            rows = pl.ds(pl.multiple_of(tile * TILE, TILE), TILE)
            total = jnp.zeros((TILE, LB), F32)
            for t in range(n_out):
                w = of[rows, t * LB : (t + 1) * LB].astype(F32)
                wide_of[rows, t * LB : (t + 1) * LB] = w
                total = total + w * w
            square[rows, :] = total
            return 0

        lax.fori_loop(first, last, one, 0)

    loads[0].wait()
    for h in range(2):
        loads[1 + h].wait()
        if h == 1:
            loads[5].start()
        partial = lax.dot_general(
            inj[...], sf[h * n_half : (h + 1) * n_half, :], (((1,), (1,)), ((), ())),
            preferred_element_type=F32,
        )
        for d in range(n_out // 2):
            parts[h * (n_out // 2) + d] = partial[:, d * LB : (d + 1) * LB]
    pl.semaphore_wait(barrier, n_out + n_line - 2)
    sent = send_parts(parts, recv_o, s_ro, "out")
    for load in loads[3:]:
        load.wait()
    hot_table(hot, line, n_out, n_k)
    widen(0, n_tiles // 2 - 1)
    slots_o[me_out] = sum_parts(parts, recv_o, sent, "out")
    sent += spread(slots_o, s_go, "out", lambda: widen(n_tiles // 2 - 1, n_tiles))
    flow = split3(jnp.concatenate([slots_o[i] for i in range(n_out)], axis=1))
    falls = [[message(picked, recv_l, s_rl, m, i, FALL_PIECES[m]) for i in range(n_line - 1)] for m in range(3)]
    for m in range(3):
        first, many = FALL_PIECES[m]
        got = add3(
            jnp.dot(flow, hot[:, first * LB : (first + many) * LB], preferred_element_type=F32)
        )
        for i in range(many):
            picked[first + i] = got[:, i * LB : (i + 1) * LB]
        for copy in falls[m]:
            copy.start()
    for t in range(n_out):
        cols = slice(t * LB, (t + 1) * LB)
        for c in range(CASES):
            low[c, :, cols] = jnp.broadcast_to(-lim[:, cols] - slots_o[t, c : c + 1, :], (8, LB))
            high[c, :, cols] = jnp.broadcast_to(lim[:, cols] - slots_o[t, c : c + 1, :], (8, LB))
    dsum[...] = jnp.zeros_like(dsum)
    ids = lax.broadcasted_iota(jnp.int32, (n_tiles, n_tiles), 0)
    place = lax.broadcasted_iota(jnp.int32, (n_tiles, n_tiles), 1)
    listed = (list_ref[...] == ids) & (place < count_ref[...])
    flags = jnp.sum(jnp.where(listed, 1.0, 0.0), axis=1, keepdims=True)
    act[...] = jnp.broadcast_to(flags, (n_tiles, LB))

    def take_falls(m):
        first, many = FALL_PIECES[m]
        for i in range(n_line - 1):
            falls[m][i].wait_recv()
        for b in range(first, first + many):
            total = picked[b]
            for i in range(n_line - 1):
                total = total + recv_l[i, b]
            slots_l[b] = total
            turned[b * LB : (b + 1) * LB, 0:CASES] = total.T

    lanes = lax.broadcasted_iota(jnp.int32, (LB, LB), 1)
    n_sub = LB // 8

    def terms_of_block(b):
        k0 = pl.multiple_of(b * LB, LB)
        rows = pl.ds(k0, LB)
        on_a = act[pl.ds(2 * b, 1), :]
        on_b = act[pl.ds(2 * b + 1, 1), :]
        on = jnp.concatenate([jnp.broadcast_to(on_a, (TILE, LB)), jnp.broadcast_to(on_b, (TILE, LB))], axis=0)
        masked = turned[rows, :] * on
        for c in range(CASES):
            fall[c] = jnp.broadcast_to(masked[:, c : c + 1], (LB, LB))

        def reduce_rows(c, sums):
            return jnp.where(lanes == c, jnp.sum(fall[jnp.maximum(c, 0)], axis=1, keepdims=True), sums)

        def case_step(c):
            ffs = [fall[c, 8 * i : 8 * i + 8, :] for i in range(n_sub)]
            acc = [ffs[i] * square[pl.ds(k0 + 8 * i, 8), :] for i in range(n_sub)]
            for t in range(n_out):
                cols = slice(t * LB, (t + 1) * LB)
                lo = low[c, :, cols]
                hi = high[c, :, cols]
                total = None
                for i in range(0, n_sub, 2):
                    pair = []
                    for j in (i, i + 1):
                        o = wide_of[pl.ds(k0 + 8 * j, 8), cols]
                        q = jnp.minimum(jnp.maximum(ffs[j] * o, lo), hi)
                        acc[j] = acc[j] - q * o
                        pair.append(q)
                    both = pair[0] + pair[1]
                    total = both if total is None else total + both
                dsum[c, :, cols] += total
            for i in range(n_sub):
                fall[c, 8 * i : 8 * i + 8, :] = acc[i]

        def group_step(g, sums):
            for e in range(GROUP):
                sums = reduce_rows(g * GROUP - GROUP + e, sums)
            for e in range(GROUP):
                case_step(g * GROUP + e)
            return sums

        sums = lax.fori_loop(0, CASES // GROUP, group_step, jnp.zeros((LB, LB), F32))
        for e in range(GROUP):
            sums = reduce_rows(CASES - GROUP + e, sums)
        rev[b] = (sums * on).T[:CASES]

    turns = [[message(rev, recv_r, s_rr, m, i, TERM_PIECES[m]) for i in range(n_line - 1)] for m in range(3)]

    def block_step(b, _):
        for m in range(3):

            @pl.when(b == FALL_PIECES[m][0])
            def _():
                take_falls(m)

        terms_of_block(b)
        for m in range(3):

            @pl.when(b == sum(TERM_PIECES[m]) - 1)
            def _():
                for copy in turns[m]:
                    copy.start()

        return 0

    lax.fori_loop(0, n_line, block_step, 0)

    falling = []
    for b in range(n_line):
        on = jnp.where(lanes[0:1] < TILE, act[2 * b : 2 * b + 1, :], act[2 * b + 1 : 2 * b + 2, :])
        falling.append(slots_l[b] * on)
    qsum = add3(jnp.dot(split3(jnp.concatenate(falling, axis=1)), of[...], preferred_element_type=F32))
    idle = TILE * (n_tiles - jnp.sum(act[...], axis=0, keepdims=True))
    for t in range(n_out):
        cols = slice(t * LB, (t + 1) * LB)
        rest = jnp.minimum(jnp.maximum(0.0, low[:, 0, cols]), high[:, 0, cols])
        terms[t] = qsum[:, cols] - (jnp.sum(dsum[:, :, cols], axis=1) - idle * rest)

    def summed(m):
        first, many = TERM_PIECES[m]
        for i in range(n_line - 1):
            turns[m][i].wait_recv()
        blocks = []
        for b in range(first, first + many):
            total = rev[b]
            for i in range(n_line - 1):
                total = total + recv_r[i, b]
            blocks.append(total)
        return blocks

    def place(three, cols):
        got = add3(
            lax.dot_general(three, hot[:, cols], (((1,), (1,)), ((), ())), preferred_element_type=F32)
        )
        for t in range(n_out):
            terms[t] += got[:, t * LB : (t + 1) * LB]

    place(split3(jnp.concatenate(summed(0) + summed(1), axis=1)), slice(0, n_k - LB))
    place(split3(summed(2)[0]), slice(n_k - LB, n_k))
    scattered = send_parts(terms, recv_t, s_rt, "out")
    grad = sum_parts(terms, recv_t, scattered, "out")
    slots_g[me_out] = (grad * (2.0 / NO)).astype(BF16)
    sent += scattered + spread(slots_g, s_gg, "out")
    rounded = jnp.concatenate([slots_g[i] for i in range(n_out)], axis=1)
    partial = jnp.dot(rounded, sf[...], preferred_element_type=F32)
    slots_f[me_line] = partial.astype(BF16)
    sent += spread(slots_f, s_gf, "line")
    result = slots_f[0].astype(F32)
    for i in range(1, n_line):
        result = result + slots_f[i].astype(F32)
    out_ref[...] = result
    for piece in falls + turns:
        finish(piece)
    finish(sent)


def shards(
    n_line, n_out, injections, shift_factors, outage_factors, limits, outage_line, tile_list, tile_count
):
    n_k = n_line * LB
    n_l = n_out * LB
    block = (CASES, LB)
    dma = pltpu.SemaphoreType.DMA
    line_row = outage_line.reshape(1, n_k)
    limit_row = limits.reshape(1, n_l)
    per_line = pltpu.VMEM((n_line,) + block, F32)
    per_out = pltpu.VMEM((n_out,) + block, F32)
    return pl.pallas_call(
        functools.partial(gradient_kernel, n_line, n_out),
        in_specs=[HBM] * 5 + [VMEM] * 2,
        out_specs=VMEM,
        out_shape=jax.ShapeDtypeStruct((CASES, shift_factors.shape[1]), F32),
        scratch_shapes=[
            pltpu.VMEM(injections.shape, BF16),
            pltpu.VMEM(shift_factors.shape, BF16),
            pltpu.VMEM(outage_factors.shape, BF16),
            pltpu.VMEM(limit_row.shape, F32),
            pltpu.VMEM(line_row.shape, jnp.int32),
            per_out,
            per_out,
            per_out,
            pltpu.VMEM((n_l, n_k), BF16),
            per_line,
            pltpu.VMEM((n_line - 1, n_line) + block, F32),
            per_line,
            pltpu.VMEM((n_k, n_l), F32),
            pltpu.VMEM((n_k, LB), F32),
            pltpu.VMEM((CASES, 8, n_l), F32),
            pltpu.VMEM((CASES, 8, n_l), F32),
            pltpu.VMEM((CASES, LB, LB), F32),
            pltpu.VMEM((CASES, 8, n_l), F32),
            pltpu.VMEM((n_k, LB), F32),
            pltpu.VMEM((n_k // TILE, LB), F32),
            per_line,
            pltpu.VMEM((n_line - 1, n_line) + block, F32),
            per_out,
            per_out,
            pltpu.VMEM((n_out,) + block, BF16),
            pltpu.VMEM((n_line, CASES, shift_factors.shape[1]), BF16),
            dma((6,)),
            dma((2, n_out)),
            dma((2, n_out)),
            dma((2, 3, n_line)),
            dma((2, 3, n_line)),
            dma((2, n_out)),
            dma((2, n_out)),
            dma((2, n_line)),
        ],
        compiler_params=pltpu.CompilerParams(
            collective_id=0, has_side_effects=True, vmem_limit_bytes=63 * 2**20
        ),
        name="gradient",
    )(injections, shift_factors, outage_factors, limit_row, line_row, tile_list, tile_count.reshape(1, 1))


def solution(mesh):
    placed = (
        P(None, "out"),
        P("line", "out"),
        P("out", "line"),
        P("line"),
        P("out"),
        P("out", None),
        P("out"),
    )
    return jax.shard_map(
        functools.partial(shards, mesh.shape["line"], mesh.shape["out"]),
        mesh=mesh,
        in_specs=placed,
        out_specs=P(None, "out"),
        check_vma=False,
    )
```
